32 devices in a mesh: copies: 2 (over y), shard: 4 (over z), dom: 4 (over x, core).
Axes of the slice: x: 2, y: 2, z: 4, core: 2. Of those that a mesh axis runs over, the one named last changes fastest.
Arguments:
- features: float32 [16384, 256], P(('copies', 'shard', 'dom')), parts along dimension 0, may hold values from -6 to 6
- weight: float32 [256, 256], replicated, may hold values from -0.375 to 0.375
- cotangent: float32 [16384, 256], P(('copies', 'shard', 'dom')), parts along dimension 0, may hold values from -6 to 6
- block_values: bfloat16 [128, 16, 128, 128], P(('copies', 'shard', 'dom')), parts along dimension 0
- block_list: int32 [128, 16], P(('copies', 'shard', 'dom')), parts along dimension 0, may hold values from 0 to 19, as said below
- send_inner: int32 [32, 4, 2], P(('copies', 'shard', 'dom')), parts along dimension 0, may hold values from -1 to 3, as said below
- send_outer: int32 [32, 4, 2], P(('copies', 'shard', 'dom')), parts along dimension 0, may hold values from -1 to 3, as said below
Outputs:
- activations: float32 [16384, 256], P(('copies', 'shard', 'dom')), parts along dimension 0
- grad_features: float32 [16384, 256], P(('copies', 'shard', 'dom')), parts along dimension 0
- grad_weight: float32 [512, 256], P('copies'), parts along dimension 0
The draws below stay inside these ranges and needn't reach their ends.
There are 2 independent parts, one for each index of `copies`. The reference program is written for one: setup_inputs(seed, part) draws one part's arguments, and reference() takes and returns one part's arrays. A program takes and returns all parts, laid end to end along the dimension named above; an argument that names none is the same for every part. Nothing has to cross between parts.
Inputs may be any that keep to these rules, and one draw needn't show every extreme that they name: `block_list`: every nonempty slot of send_inner and send_outer is named exactly once on the receiving device, and no empty slot is named. Values below 4 name local row blocks. `send_inner`: -1 marks an empty slot; nonempty slots come first; a device sends nothing to itself; in every partition one device receives 2 row blocks from each other device of it. `send_outer`: -1 marks an empty slot; nonempty slots come first; nothing goes to the own partition; for every shard index one partition receives 2 row blocks from each other partition.
All inputs are finite; a program needn't handle non-finite values.
Results may differ from the reference program's by a relative error of at most 0.0033.
Values may be sent and summed in bfloat16 or wider, within the bound.
No kernel may reach another device: no remote copies, remote signals or barrier semaphores. Data moves between devices by JAX's collectives and lax.ppermute only.
A program may use at most 128 MiB of HBM per device.

```python
import math
import jax
import jax.numpy as jnp
from jax import lax

F = 256
BS = 128
ROWB = 4
K = 16
CAP_IN = 2
CAP_OUT = 2
GROUP = 16
BLOCKS = 64
NODES = 8192
N_SHARD = 4
N_DOM = 4


def routing_tables(key):
    keys = jax.random.split(key, 8)
    shard_ids = jnp.arange(N_SHARD, dtype=jnp.int32)
    dom_ids = jnp.arange(N_DOM, dtype=jnp.int32)
    inner_count = jax.random.randint(keys[0], (N_SHARD, N_DOM, N_SHARD), 0, CAP_IN + 1)
    inner_full = jax.random.randint(keys[1], (N_DOM,), 0, N_SHARD)
    inner_count = jnp.where(shard_ids[:, None, None] == inner_full[None, :, None], CAP_IN, inner_count)
    inner_count = jnp.where(shard_ids[:, None, None] == shard_ids[None, None, :], 0, inner_count)
    outer_count = jax.random.randint(keys[2], (N_SHARD, N_DOM, N_DOM), 0, CAP_OUT + 1)
    outer_full = jax.random.randint(keys[3], (N_SHARD,), 0, N_DOM)
    outer_count = jnp.where(dom_ids[None, :, None] == outer_full[:, None, None], CAP_OUT, outer_count)
    outer_count = jnp.where(dom_ids[None, :, None] == dom_ids[None, None, :], 0, outer_count)
    inner_used = jnp.arange(CAP_IN, dtype=jnp.int32)[None, None, None, :] < inner_count[..., None]
    outer_used = jnp.arange(CAP_OUT, dtype=jnp.int32)[None, None, None, :] < outer_count[..., None]
    slot_total = N_SHARD * CAP_IN + N_DOM * CAP_OUT
    positions = ROWB * K
    used = jnp.concatenate([inner_used.reshape(N_SHARD, N_DOM, N_SHARD * CAP_IN), outer_used.reshape(N_SHARD, N_DOM, N_DOM * CAP_OUT)], axis=-1).astype(jnp.int32)
    order = jnp.argsort(1 - used, axis=-1, stable=True).astype(jnp.int32)
    order = jnp.pad(order, ((0, 0), (0, 0), (0, positions - slot_total)))
    live = jnp.sum(used, axis=-1, keepdims=True)
    places = jnp.arange(positions, dtype=jnp.int32)[None, None, :]
    local_pick = jax.random.randint(keys[4], (N_SHARD, N_DOM, positions), 0, ROWB)
    codes = jnp.where(places < live, ROWB + order, local_pick)
    scores = jax.random.randint(keys[5], (N_SHARD, N_DOM, positions), 0, 2 ** 20) * positions + places
    shuffle = jnp.argsort(scores, axis=-1)
    inverse = jnp.argsort(shuffle, axis=-1)
    block_list = jnp.take_along_axis(codes, inverse, axis=-1).reshape(N_SHARD * N_DOM * ROWB, K).astype(jnp.int32)
    inner_pick = jax.random.randint(keys[6], (N_SHARD, N_DOM, N_SHARD, CAP_IN), 0, ROWB)
    count_sender = jnp.transpose(inner_count, (2, 1, 0))
    slots_in = jnp.arange(CAP_IN, dtype=jnp.int32)[None, None, None, :]
    send_inner = jnp.where(slots_in < count_sender[..., None], inner_pick, -1).reshape(N_SHARD * N_DOM, N_SHARD, CAP_IN).astype(jnp.int32)
    outer_pick = jax.random.randint(keys[7], (N_SHARD, N_DOM, N_DOM, CAP_OUT), 0, ROWB)
    count_source = jnp.transpose(outer_count, (0, 2, 1))
    slots_out = jnp.arange(CAP_OUT, dtype=jnp.int32)[None, None, None, :]
    send_outer = jnp.where(slots_out < count_source[..., None], outer_pick, -1).reshape(N_SHARD * N_DOM, N_DOM, CAP_OUT).astype(jnp.int32)
    return (block_list, send_inner, send_outer)


def draw_block_list(key, part):
    return routing_tables(key)[0]


def draw_send_inner(key, part):
    return routing_tables(key)[1]


def draw_send_outer(key, part):
    return routing_tables(key)[2]


def scaled_values(base, key, lowest, highest):
    row_key, column_key = jax.random.split(key)
    row_scale = jnp.exp(jax.random.uniform(row_key, (BLOCKS, 1, BS, 1), jnp.float32, math.log(lowest), math.log(highest)))
    column_scale = jnp.exp(jax.random.uniform(column_key, (BLOCKS, K, 1, BS), jnp.float32, math.log(0.3), math.log(3.0)))
    return (base * row_scale * column_scale).astype(jnp.bfloat16)


def draw_block_values(key, part):
    key = jax.random.fold_in(key, 17)
    base_key, scale_key = jax.random.split(key)
    shape = (BLOCKS, K, BS, BS)
    base = jnp.clip(jax.random.normal(base_key, shape, jnp.float32), -4.0, 4.0)
    return scaled_values(base, scale_key, 0.02, 0.2)


def shard_levels(own_key, extent, shards, low, largest):
    level = 1.0
    for position, shards_of in shards:
        steps = jax.random.uniform(jax.random.fold_in(jax.random.fold_in(own_key, 6), position), (shards_of,), jnp.float32, low / len(shards), largest / len(shards))
        level = level * jnp.repeat(jnp.exp(steps), extent[position] // shards_of).reshape((-1,) + (1,) * (len(extent) - 1 - position))
    return level


def centred(rng, shape, spread, reach, pieces=(), held_as=jnp.bfloat16):
    entries = jax.random.normal(rng, shape, jnp.float32) * spread
    if len(pieces) > 0:
        entries = shard_levels(rng, shape, pieces, -0.22, 0.18) * entries
    return jnp.clip(entries, min=-reach, max=reach).astype(held_as)


def setup_inputs(seed: int = 0, part: int = 0) -> dict:
    streams_of = jax.random.split(jax.random.key(seed), 8)
    part_splits = jax.random.split(jax.random.fold_in(streams_of[7], part), 8)
    return {
        "features": centred(part_splits[0], (NODES, F), 1.0, 6.0, ((0, 16),), jnp.float32),
        "weight": centred(streams_of[1], (F, F), F ** -0.5, 0.375, (), jnp.float32),
        "cotangent": centred(part_splits[2], (NODES, F), 1.0, 6.0, ((0, 16),), jnp.float32),
        "block_values": draw_block_values(jax.random.fold_in(jax.random.fold_in(streams_of[7], part), 71), part),
        "block_list": draw_block_list(jax.random.fold_in(jax.random.fold_in(streams_of[7], part), 71), part),
        "send_inner": draw_send_inner(jax.random.fold_in(jax.random.fold_in(streams_of[7], part), 71), part),
        "send_outer": draw_send_outer(jax.random.fold_in(jax.random.fold_in(streams_of[7], part), 71), part),
    }


def source_table(block_list, send_inner, send_outer):
    shard_ids = jnp.arange(N_SHARD, dtype=jnp.int32)
    dom_ids = jnp.arange(N_DOM, dtype=jnp.int32)
    device = shard_ids[:, None, None] * N_DOM + dom_ids[None, :, None]
    local_src = device * ROWB + jnp.arange(ROWB, dtype=jnp.int32)[None, None, :]
    inner = jnp.transpose(send_inner.reshape(N_SHARD, N_DOM, N_SHARD, CAP_IN), (2, 1, 0, 3))
    inner_dev = shard_ids[None, None, :, None] * N_DOM + dom_ids[None, :, None, None]
    inner_src = (inner_dev * ROWB + jnp.maximum(inner, 0)).reshape(N_SHARD, N_DOM, N_SHARD * CAP_IN)
    outer = jnp.transpose(send_outer.reshape(N_SHARD, N_DOM, N_DOM, CAP_OUT), (0, 2, 1, 3))
    outer_dev = shard_ids[:, None, None, None] * N_DOM + dom_ids[None, None, :, None]
    outer_src = (outer_dev * ROWB + jnp.maximum(outer, 0)).reshape(N_SHARD, N_DOM, N_DOM * CAP_OUT)
    table = jnp.concatenate([local_src, inner_src, outer_src], axis=-1).astype(jnp.int32)
    listed = block_list.reshape(N_SHARD, N_DOM, ROWB * K).astype(jnp.int32)
    chosen = jnp.take_along_axis(table, listed, axis=-1)
    return chosen.reshape(GROUP, ROWB, K).astype(jnp.int32)

def reference(features, weight, cotangent, block_values, block_list, send_inner, send_outer):
    highest = lax.Precision.HIGHEST
    projected = jnp.dot(features, weight, precision=highest, preferred_element_type=jnp.float32)
    half_blocks = projected.astype(jnp.bfloat16).reshape(BLOCKS, BS, F)
    source_block = source_table(block_list, send_inner, send_outer)
    grouped_values = block_values.reshape(GROUP, ROWB, K, BS, BS)

    def forward_group(items):
        values, sources = items
        picked = half_blocks[sources]
        values_wide = values.astype(jnp.float32)
        summed = jnp.einsum('rkab,rkbf->raf', values_wide, picked.astype(jnp.float32))
        squares = lax.optimization_barrier(jnp.sum(values_wide * values_wide, axis=(1, 3)))
        return (summed, squares)
    summed, squares = lax.map(forward_group, (grouped_values, source_block))
    row_scale = jnp.sqrt(1.0 + squares.reshape(NODES, 1))
    mixed = (projected + summed.reshape(NODES, F)) / row_scale
    logistic = jax.nn.sigmoid(mixed)
    activations = mixed * logistic
    grad_mixed = cotangent * logistic * (1.0 + mixed * (1.0 - logistic))
    scaled = grad_mixed / row_scale
    scaled_half = scaled.astype(jnp.bfloat16).reshape(GROUP, ROWB, BS, F)

    def backward_step(carry, items):
        values, sources, rows_half = items
        terms = jnp.einsum('rkab,raf->rkbf', values.astype(jnp.float32), rows_half.astype(jnp.float32))
        carry = carry.at[sources.reshape(-1)].add(terms.reshape(ROWB * K, BS, F))
        return (carry, None)
    gathered, _ = lax.scan(backward_step, jnp.zeros((BLOCKS, BS, F), jnp.float32), (grouped_values, source_block, scaled_half))
    grad_projected = scaled + gathered.reshape(NODES, F)
    grad_weight = jnp.dot(features.T, grad_projected, precision=highest, preferred_element_type=jnp.float32)
    grad_features = jnp.dot(grad_projected, weight.T, precision=highest, preferred_element_type=jnp.float32)
    return (activations, grad_features, grad_weight)
```

```python
import functools
import jax
import jax.numpy as jnp
from jax import lax
from jax.experimental import pallas as pl
from jax.experimental.pallas import tpu as pltpu
from jax.sharding import PartitionSpec as P

F32 = jnp.float32
BF16 = jnp.bfloat16
VMEM = pl.BlockSpec(memory_space=pltpu.VMEM)
SMEM = pl.BlockSpec(memory_space=pltpu.SMEM)
PARAMS = pltpu.CompilerParams(vmem_limit_bytes=48 * 1024 * 1024)


def partner(i, k, n):
    if n & (n - 1) == 0:
        return i ^ k
    return (i + k) % n


def back_partner(i, k, n):
    if n & (n - 1) == 0:
        return i ^ k
    return (i + n - k) % n


def exchange_order(n):
    return sorted(range(1, n), key=lambda k: -k)


def send(x, axis, k, n):
    return lax.ppermute(x, axis, [(i, partner(i, k, n)) for i in range(n)])


def send_back(x, axis, k, n):
    return lax.ppermute(x, axis, [(i, back_partner(i, k, n)) for i in range(n)])


def split(x):
    hi = x.astype(BF16)
    return hi, (x - hi.astype(F32)).astype(BF16)


def mm(a, b, dims=((1,), (0,))):
    return lax.dot_general(a, b, (dims, ((), ())), preferred_element_type=F32)


def mm3(a, b, dims=((1,), (0,))):
    ah, al = a
    bh, bl = b
    return mm(ah, bh, dims) + (mm(ah, bl, dims) + mm(al, bh, dims))


def call(kernel, out_shape, flops, nbytes, in_specs, out_specs, scratch=()):
    return pl.pallas_call(
        kernel,
        out_shape=out_shape,
        in_specs=in_specs,
        out_specs=out_specs,
        scratch_shapes=list(scratch),
        compiler_params=PARAMS,
        cost_estimate=pl.CostEstimate(flops=flops, bytes_accessed=nbytes, transcendentals=0),
    )


def pack_kernel(axis, n, side, targets_ref, features_ref, *out_refs):
    me = lax.axis_index(axis)
    cap = targets_ref.shape[2]
    for out_ref, k in zip(out_refs, exchange_order(n)):
        peer = partner(me, k, n)
        for j in range(cap):
            target = targets_ref[0, peer, j]
            row = pl.multiple_of(jnp.maximum(target, 0) * side, side)
            rows = features_ref[pl.ds(row, side), :]
            out_ref[j * side : (j + 1) * side, :] = jnp.where(target >= 0, rows, 0.0).astype(BF16)


def slot_codes(row_blocks, ns, nd, inner_cap, outer_cap):
    s = lax.axis_index("shard")
    p = lax.axis_index("dom")
    codes = []
    for k in exchange_order(ns):
        for j in range(inner_cap):
            codes.append(row_blocks + back_partner(s, k, ns) * inner_cap + j)
    for k in exchange_order(nd):
        for j in range(outer_cap):
            codes.append(row_blocks + ns * inner_cap + back_partner(p, k, nd) * outer_cap + j)
    return codes


def local_kernel(
    dims, list_ref, features_ref, weight_ref, values_ref,
    base_ref, local_ref, scale_ref, picked_ref, turned_ref, place_ref,
    sources_ref, inverse_ref,
):
    row_blocks, fanout, side, width, ns, nd, inner_cap, outer_cap = dims
    codes = row_blocks + ns * inner_cap + nd * outer_cap
    for c in range(codes):
        inverse_ref[c] = 0
    for n in range(row_blocks * fanout):
        inverse_ref[list_ref[n // fanout, n % fanout]] = n
    for i, code in enumerate(slot_codes(row_blocks, ns, nd, inner_cap, outer_cap)):
        n = inverse_ref[code]
        r = n // fanout
        place_ref[i] = r
        block = values_ref[r, n % fanout]
        picked_ref[i] = block
        turned_ref[i] = block.T
    fh, fl = split(features_ref[...])
    projected = mm3((fh, fl), split(weight_ref[...]))
    sources_ref[: row_blocks * side, :width] = projected.astype(BF16)
    sources_ref[: row_blocks * side, width : 2 * width] = fh
    sources_ref[: row_blocks * side, 2 * width :] = fl
    sources_ref[row_blocks * side :, :] = jnp.zeros((side, 3 * width), BF16)
    for r in range(row_blocks):
        rows = slice(r * side, (r + 1) * side)
        squares = jnp.zeros((side, side), F32)
        for k in range(fanout):
            block = values_ref[r, k].astype(F32)
            squares = squares + block * block
        scale = lax.rsqrt(1.0 + jnp.sum(squares, axis=1, keepdims=True))
        scale_ref[rows, :] = jnp.broadcast_to(scale, (side, width))
        total = jnp.zeros((side, 3 * width), F32)
        for k in range(0, fanout, 2):
            blocks = jnp.concatenate([values_ref[r, k], values_ref[r, k + 1]], axis=1)
            picks = []
            for kk in (k, k + 1):
                at = pl.multiple_of(jnp.minimum(list_ref[r, kk], row_blocks) * side, side)
                picks.append(sources_ref[pl.ds(at, side), :])
            total = total + mm(blocks, jnp.concatenate(picks, axis=0))
        base_ref[rows, :] = projected[rows, :] + total[:, :width]
        local_ref[rows, :] = total[:, width : 2 * width] + total[:, 2 * width :]


def middle_kernel(dims, place_ref, *refs):
    row_blocks, fanout, side, width, ns, nd, inner_cap, outer_cap = dims
    n_in = (ns - 1) + (nd - 1)
    arrived = refs[:n_in]
    base_ref, scale_ref, picked_ref, turned_ref, weight_ref, cotangent_ref = refs[n_in : n_in + 6]
    act_ref, scaled_ref, half_ref, total_ref = refs[n_in + 6 : n_in + 10]
    leaving = refs[n_in + 10 :]
    total_ref[...] = jnp.zeros_like(total_ref)
    i = 0
    for ref in arrived:
        for j in range(ref.shape[0] // side):
            term = mm(picked_ref[i], ref[j * side : (j + 1) * side, :])
            rows = pl.ds(pl.multiple_of(place_ref[i] * side, side), side)
            total_ref[rows, :] += term
            i += 1
    weight = split(weight_ref[...])
    for r in range(row_blocks):
        rows = slice(r * side, (r + 1) * side)
        scale = scale_ref[rows, :]
        mixed = (base_ref[rows, :] + mm3(split(total_ref[rows, :]), weight)) * scale
        gate = jax.nn.sigmoid(mixed)
        act_ref[rows, :] = mixed * gate
        scaled = cotangent_ref[rows, :] * gate * (1.0 + mixed * (1.0 - gate)) * scale
        scaled_ref[rows, :] = scaled
        half_ref[rows, :] = scaled.astype(BF16)
    i = 0
    for ref in leaving:
        for j in range(ref.shape[0] // side):
            rows = pl.ds(pl.multiple_of(place_ref[i] * side, side), side)
            ref[j * side : (j + 1) * side, :] = mm(turned_ref[i], half_ref[rows, :]).astype(BF16)
            i += 1


def weight_kernel(nd, features_ref, local_ref, total_ref, scaled_ref, half_ref, *out_refs):
    p = lax.axis_index("dom")
    down = ((0,), (0,))
    ah, al = split(local_ref[...] + total_ref[...])
    half = half_ref[...]
    term = mm3(split(features_ref[...]), split(scaled_ref[...]), down)
    term = term + (mm(ah, half, down) + mm(al, half, down))
    scratch_ref = out_refs[-1]
    scratch_ref[...] = term
    piece = term.shape[0] // nd
    for out_ref, k in zip(out_refs[:-1], [0] + exchange_order(nd)):
        at = pl.multiple_of(partner(p, k, nd) * piece, 8)
        out_ref[...] = scratch_ref[pl.ds(at, piece), :]


def spread_kernel(dims, list_ref, values_ref, scaled_ref, half_ref, weight_ref, out_ref, sums_ref):
    row_blocks, fanout, side, width = dims
    sums_ref[...] = jnp.zeros_like(sums_ref)
    for r in range(row_blocks):
        half = half_ref[r * side : (r + 1) * side, :]
        for k in range(fanout):
            at = pl.multiple_of(jnp.minimum(list_ref[r, k], row_blocks) * side, side)
            sums_ref[pl.ds(at, side), :] += mm(values_ref[r, k], half, ((0,), (0,)))
    grad = scaled_ref[...] + sums_ref[: row_blocks * side, :]
    out_ref[...] = mm3(split(grad), split(weight_ref[...]), ((1,), (1,)))


def finish_kernel(ns, nd, side, inner_ref, outer_ref, weight_ref, part_ref, *refs):
    arrived, out_ref, sums_ref = refs[:-2], refs[-2], refs[-1]
    sums_ref[...] = jnp.zeros_like(sums_ref)
    slots = []
    for axis, n, targets_ref in (("shard", ns, inner_ref), ("dom", nd, outer_ref)):
        me = lax.axis_index(axis)
        for k in exchange_order(n):
            slots.append((targets_ref, partner(me, k, n)))
    for ref, (targets_ref, peer) in zip(arrived, slots):
        for j in range(ref.shape[0] // side):
            target = targets_ref[0, peer, j]
            rows = pl.ds(pl.multiple_of(jnp.maximum(target, 0) * side, side), side)
            term = ref[j * side : (j + 1) * side, :].astype(F32)
            sums_ref[rows, :] += jnp.where(target >= 0, term, 0.0)
    out_ref[...] = part_ref[...] + mm3(split(sums_ref[...]), split(weight_ref[...]), ((1,), (1,)))


def add_kernel(*refs):
    total = refs[0][...]
    for ref in refs[1:-1]:
        total = total + ref[...]
    refs[-1][...] = total


def place_kernel(nd, *refs):
    p = lax.axis_index("dom")
    out_ref = refs[-1]
    piece = refs[0].shape[0]
    for ref, k in zip(refs[:-1], [0] + exchange_order(nd)):
        at = pl.multiple_of(back_partner(p, k, nd) * piece, 8)
        out_ref[pl.ds(at, piece), :] = ref[...]


def on_device(features, weight, cotangent, block_values, block_list, send_inner, send_outer):
    node_count, width = features.shape
    row_blocks, fanout, side, _ = block_values.shape
    ns = lax.axis_size("shard")
    nd = lax.axis_size("dom")
    inner_cap = send_inner.shape[2]
    outer_cap = send_outer.shape[2]
    slots = (ns - 1) * inner_cap + (nd - 1) * outer_cap
    dims = (row_blocks, fanout, side, width, ns, nd, inner_cap, outer_cap)
    shape = jax.ShapeDtypeStruct
    rows_f32 = shape((node_count, width), F32)
    rows_f16 = shape((node_count, width), BF16)
    packed_inner = [shape((inner_cap * side, width), BF16)] * (ns - 1)
    packed_outer = [shape((outer_cap * side, width), BF16)] * (nd - 1)
    nbytes = node_count * width * 4

    def pack(axis, n, targets, shapes):
        return call(
            functools.partial(pack_kernel, axis, n, side), shapes, 0, 3 * nbytes,
            [SMEM, VMEM], [VMEM] * len(shapes),
        )(targets, features)

    inner_out = pack("shard", ns, send_inner, packed_inner)
    inner_in = [send(x, "shard", k, ns) for x, k in zip(inner_out, exchange_order(ns))]
    outer_out = pack("dom", nd, send_outer, packed_outer)
    outer_in = [send(x, "dom", k, nd) for x, k in zip(outer_out, exchange_order(nd))]

    base, local, scale, picked, turned, place = call(
        functools.partial(local_kernel, dims),
        [
            rows_f32, rows_f32, rows_f32,
            shape((slots, side, side), BF16), shape((slots, side, side), BF16), shape((slots,), jnp.int32),
        ],
        4 * row_blocks * fanout * side * side * width * 3, 12 * nbytes,
        [SMEM, VMEM, VMEM, VMEM], [VMEM] * 5 + [SMEM],
        [
            pltpu.VMEM(((row_blocks + 1) * side, 3 * width), BF16),
            pltpu.SMEM((row_blocks + ns * inner_cap + nd * outer_cap,), jnp.int32),
        ],
    )(block_list, features, weight, block_values)

    n_in = ns - 1 + nd - 1
    outs = call(
        functools.partial(middle_kernel, dims),
        [rows_f32, rows_f32, rows_f16, rows_f32] + packed_inner + packed_outer,
        2 * slots * side * side * width * 2, 8 * nbytes,
        [SMEM] + [VMEM] * (n_in + 6), [VMEM] * (4 + n_in),
    )(place, *inner_in, *outer_in, base, scale, picked, turned, weight, cotangent)
    activations, scaled, half, total = outs[:4]
    inner_terms, outer_terms = outs[4 : 4 + ns - 1], outs[4 + ns - 1 :]

    inner_back = [send_back(x, "shard", k, ns) for x, k in zip(inner_terms, exchange_order(ns))]
    piece = shape((width // nd, width), F32)
    pieces = call(
        functools.partial(weight_kernel, nd),
        [piece] * nd, 10 * node_count * width * width, 5 * nbytes,
        [VMEM] * 5, [VMEM] * nd, [pltpu.VMEM((width, width), F32)],
    )(features, local, total, scaled, half)
    outer_back = [send_back(x, "dom", k, nd) for x, k in zip(outer_terms, exchange_order(nd))]

    add = lambda xs: call(
        add_kernel, piece, 0, len(xs) * nbytes // 8, [VMEM] * len(xs), VMEM
    )(*xs)
    weight_sum = add([pieces[0]] + [send(x, "dom", k, nd) for x, k in zip(pieces[1:], exchange_order(nd))])
    weight_sum = add([weight_sum] + [send(weight_sum, "shard", k, ns) for k in exchange_order(ns)])
    gathered = [weight_sum] + [send(weight_sum, "dom", k, nd) for k in exchange_order(nd)]
    grad_weight = call(
        functools.partial(place_kernel, nd), shape((width, width), F32), 0, nbytes,
        [VMEM] * nd, VMEM,
    )(*gathered)

    part = call(
        functools.partial(spread_kernel, dims[:4]), rows_f32,
        2 * row_blocks * fanout * side * side * width, 8 * nbytes,
        [SMEM] + [VMEM] * 4, VMEM, [pltpu.VMEM(((row_blocks + 1) * side, width), F32)],
    )(block_list, block_values, scaled, half, weight)
    grad_features = call(
        functools.partial(finish_kernel, ns, nd, side), rows_f32,
        6 * node_count * width * width, 4 * nbytes,
        [SMEM, SMEM] + [VMEM] * (2 + n_in), VMEM, [pltpu.VMEM((node_count, width), F32)],
    )(send_inner, send_outer, weight, part, *inner_back, *outer_back)
    return (activations, grad_features, grad_weight)


def solution(mesh):
    rows = ("copies", "shard", "dom")
    return jax.shard_map(
        on_device,
        mesh=mesh,
        in_specs=(
            P(rows, None),
            P(),
            P(rows, None),
            P(rows, None, None, None),
            P(rows, None),
            P(rows, None, None),
            P(rows, None, None),
        ),
        out_specs=(P(rows, None), P(rows, None), P("copies", None)),
        check_vma=False,
    )
```

```python
import functools
import jax
import jax.numpy as jnp
from jax import lax
from jax.experimental import pallas as pl
from jax.experimental.pallas import tpu as pltpu
from jax.sharding import PartitionSpec as P

F32 = jnp.float32
BF16 = jnp.bfloat16
VMEM = pl.BlockSpec(memory_space=pltpu.VMEM)
SMEM = pl.BlockSpec(memory_space=pltpu.SMEM)
HBM = pl.BlockSpec(memory_space=pltpu.HBM)
PARAMS = pltpu.CompilerParams(vmem_limit_bytes=48 * 1024 * 1024)


def partner(i, k, n):
    if n & (n - 1) == 0:
        return i ^ k
    return (i + k) % n


def back_partner(i, k, n):
    if n & (n - 1) == 0:
        return i ^ k
    return (i + n - k) % n


def exchange_order(n):
    return sorted(range(1, n), key=lambda k: -k)


def send(x, axis, k, n):
    return lax.ppermute(x, axis, [(i, partner(i, k, n)) for i in range(n)])


def send_back(x, axis, k, n):
    return lax.ppermute(x, axis, [(i, back_partner(i, k, n)) for i in range(n)])


def split(x):
    hi = x.astype(BF16)
    return hi, (x - hi.astype(F32)).astype(BF16)


def mm(a, b, dims=((1,), (0,))):
    return lax.dot_general(a, b, (dims, ((), ())), preferred_element_type=F32)


def mm3(a, b, dims=((1,), (0,))):
    ah, al = a
    bh, bl = b
    return mm(ah, bh, dims) + (mm(ah, bl, dims) + mm(al, bh, dims))


def call(kernel, out_shape, flops, nbytes, in_specs, out_specs, scratch=()):
    return pl.pallas_call(
        kernel,
        out_shape=out_shape,
        in_specs=in_specs,
        out_specs=out_specs,
        scratch_shapes=list(scratch),
        compiler_params=PARAMS,
        cost_estimate=pl.CostEstimate(flops=flops, bytes_accessed=nbytes, transcendentals=0),
    )


def fetch(pairs, sems):
    copies = [pltpu.make_async_copy(src, dst, sems.at[i]) for i, (src, dst) in enumerate(pairs)]
    for copy in copies:
        copy.start()
    return copies


def pack_rows(out_ref, targets_ref, peer, rows_ref, side):
    for j in range(targets_ref.shape[1]):
        target = targets_ref[0, j, peer]
        rows = rows_ref[pl.ds(pl.multiple_of(jnp.maximum(target, 0) * side, side), side), :]
        out_ref[j * side : (j + 1) * side, :] = jnp.where(target >= 0, rows, 0.0).astype(BF16)


def pack_kernel(ns, nd, side, inner_hbm, outer_hbm, features_hbm, *refs):
    out_refs, (inner_ref, outer_ref, rows_ref, sems) = refs[:-4], refs[-4:]
    half = rows_ref.shape[0] // 2
    copies = fetch(
        [
            (inner_hbm, inner_ref),
            (outer_hbm, outer_ref),
            (features_hbm.at[:half], rows_ref.at[:half]),
            (features_hbm.at[half:], rows_ref.at[half:]),
        ],
        sems,
    )
    for copy in copies:
        copy.wait()
    s = lax.axis_index("shard")
    p = lax.axis_index("dom")
    plan = [(inner_ref, partner(s, k, ns)) for k in exchange_order(ns)]
    plan += [(outer_ref, partner(p, k, nd)) for k in exchange_order(nd)[:-1]]
    for out_ref, (targets_ref, peer) in zip(out_refs, plan):
        pack_rows(out_ref, targets_ref, peer, rows_ref, side)


def slot_codes(row_blocks, ns, nd, inner_cap, outer_cap):
    s = lax.axis_index("shard")
    p = lax.axis_index("dom")
    codes = []
    for k in exchange_order(ns):
        for j in range(inner_cap):
            codes.append(row_blocks + back_partner(s, k, ns) * inner_cap + j)
    for k in exchange_order(nd):
        for j in range(outer_cap):
            codes.append(row_blocks + ns * inner_cap + back_partner(p, k, nd) * outer_cap + j)
    return codes


def local_kernel(
    dims, list_hbm, outer_hbm, features_hbm, weight_hbm, values_hbm,
    near_ref, base_ref, local_ref, scale_ref, picked_ref, turned_ref, place_ref,
    list_ref, outer_ref, features_ref, weight_ref, values_ref, sources_ref, inverse_ref, sems,
):
    row_blocks, fanout, side, width, ns, nd, inner_cap, outer_cap = dims
    pairs = [
        (list_hbm, list_ref), (outer_hbm, outer_ref), (features_hbm, features_ref), (weight_hbm, weight_ref)
    ]
    pairs += [(values_hbm.at[r], values_ref.at[r]) for r in range(row_blocks)]
    copies = fetch(pairs, sems)
    for copy in copies[:4]:
        copy.wait()
    pack_rows(near_ref, outer_ref, partner(lax.axis_index("dom"), exchange_order(nd)[-1], nd), features_ref, side)
    codes = row_blocks + ns * inner_cap + nd * outer_cap
    for c in range(codes):
        inverse_ref[c] = 0
    for n in range(row_blocks * fanout):
        inverse_ref[list_ref[n // fanout, n % fanout]] = n
    fh, fl = split(features_ref[...])
    projected = mm3((fh, fl), split(weight_ref[...]))
    sources_ref[: row_blocks * side, :width] = projected.astype(BF16)
    sources_ref[: row_blocks * side, width : 2 * width] = fh
    sources_ref[: row_blocks * side, 2 * width :] = fl
    sources_ref[row_blocks * side :, :] = jnp.zeros((side, 3 * width), BF16)
    for copy in copies[4:]:
        copy.wait()
    for r in range(row_blocks):
        rows = slice(r * side, (r + 1) * side)
        squares = jnp.zeros((side, side), F32)
        for k in range(fanout):
            block = values_ref[r, k].astype(F32)
            squares = squares + block * block
        scale = lax.rsqrt(1.0 + jnp.sum(squares, axis=1, keepdims=True))
        scale_ref[rows, :] = jnp.broadcast_to(scale, (side, width))
        total = jnp.zeros((side, 3 * width), F32)
        for k in range(0, fanout, 2):
            blocks = jnp.concatenate([values_ref[r, k], values_ref[r, k + 1]], axis=1)
            picks = []
            for kk in (k, k + 1):
                at = pl.multiple_of(jnp.minimum(list_ref[r, kk], row_blocks) * side, side)
                picks.append(sources_ref[pl.ds(at, side), :])
            total = total + mm(blocks, jnp.concatenate(picks, axis=0))
        base_ref[rows, :] = projected[rows, :] + total[:, :width]
        local_ref[rows, :] = total[:, width : 2 * width] + total[:, 2 * width :]
    for i, code in enumerate(slot_codes(row_blocks, ns, nd, inner_cap, outer_cap)):
        n = inverse_ref[code]
        r = n // fanout
        place_ref[i] = r
        block = values_ref[r, n % fanout]
        picked_ref[i] = block
        turned_ref[i] = block.T


def middle_kernel(dims, place_ref, *refs):
    row_blocks, fanout, side, width, ns, nd, inner_cap, outer_cap = dims
    n_in = (ns - 1) + (nd - 1)
    arrived = refs[:n_in]
    base_ref, scale_ref, picked_ref, turned_ref, weight_ref, cotangent_ref = refs[n_in : n_in + 6]
    act_ref, scaled_ref, half_ref, total_ref = refs[n_in + 6 : n_in + 10]
    leaving = refs[n_in + 10 :]
    total_ref[...] = jnp.zeros_like(total_ref)
    i = 0
    for ref in arrived:
        for j in range(ref.shape[0] // side):
            term = mm(picked_ref[i], ref[j * side : (j + 1) * side, :])
            rows = pl.ds(pl.multiple_of(place_ref[i] * side, side), side)
            total_ref[rows, :] += term
            i += 1
    weight = split(weight_ref[...])
    for r in range(row_blocks):
        rows = slice(r * side, (r + 1) * side)
        scale = scale_ref[rows, :]
        mixed = (base_ref[rows, :] + mm3(split(total_ref[rows, :]), weight)) * scale
        gate = jax.nn.sigmoid(mixed)
        act_ref[rows, :] = mixed * gate
        scaled = cotangent_ref[rows, :] * gate * (1.0 + mixed * (1.0 - gate)) * scale
        scaled_ref[rows, :] = scaled
        half_ref[rows, :] = scaled.astype(BF16)
    i = 0
    for ref in leaving:
        for j in range(inner_cap):
            rows = pl.ds(pl.multiple_of(place_ref[i] * side, side), side)
            ref[j * side : (j + 1) * side, :] = mm(turned_ref[i], half_ref[rows, :]).astype(BF16)
            i += 1


def weight_kernel(
    dims, first, place_ref, features_ref, local_ref, total_ref, scaled_ref, half_ref, turned_ref, own_ref, *refs
):
    row_blocks, fanout, side, width, ns, nd, inner_cap, outer_cap = dims
    leaving, term_ref = refs[:-1], refs[-1]
    p = lax.axis_index("dom")
    down = ((0,), (0,))
    ah, al = split(local_ref[...] + total_ref[...])
    half = half_ref[...]
    term = mm3(split(features_ref[...]), split(scaled_ref[...]), down)
    term_ref[...] = term + (mm(ah, half, down) + mm(al, half, down))
    piece = own_ref.shape[0]
    own_ref[...] = term_ref[pl.ds(pl.multiple_of(p * piece, 8), piece), :]
    i = first
    for ref, k in zip(leaving, exchange_order(nd)):
        for j in range(outer_cap):
            rows = pl.ds(pl.multiple_of(place_ref[i] * side, side), side)
            ref[j * side : (j + 1) * side, :] = mm(turned_ref[i], half_ref[rows, :]).astype(BF16)
            i += 1
        at = pl.multiple_of(back_partner(p, k, nd) * piece, 8)
        hi, lo = split(term_ref[pl.ds(at, piece), :])
        ref[outer_cap * side : outer_cap * side + piece, :] = hi
        ref[outer_cap * side + piece :, :] = lo


def spread_kernel(dims, list_hbm, values_hbm, scaled_ref, half_ref, out_ref, list_ref, values_ref, sums_ref, sems):
    row_blocks, fanout, side, width = dims
    copies = fetch(
        [(list_hbm, list_ref)] + [(values_hbm.at[r], values_ref.at[r]) for r in range(row_blocks)], sems
    )
    sums_ref[: row_blocks * side, :] = scaled_ref[...]
    copies[0].wait()
    for r in range(row_blocks):
        copies[r + 1].wait()
        half = half_ref[r * side : (r + 1) * side, :]
        for k in range(fanout):
            at = pl.multiple_of(jnp.minimum(list_ref[r, k], row_blocks) * side, side)
            sums_ref[pl.ds(at, side), :] += mm(values_ref[r, k], half, ((0,), (0,)))
    out_ref[...] = sums_ref[: row_blocks * side, :]


def tree_sum(terms):
    while len(terms) > 1:
        terms = [sum(terms[i : i + 2][1:], terms[i]) for i in range(0, len(terms), 2)]
    return terms[0]


def add_rows(sums_ref, ref, targets_ref, peer, side):
    for j in range(targets_ref.shape[1]):
        target = targets_ref[0, j, peer]
        rows = pl.ds(pl.multiple_of(jnp.maximum(target, 0) * side, side), side)
        term = ref[j * side : (j + 1) * side, :].astype(F32)
        sums_ref[rows, :] += jnp.where(target >= 0, term, 0.0)


def dom_sum_kernel(nd, side, targets_ref, part_ref, own_ref, *refs):
    arrived, (sums_ref, piece_ref) = refs[:-2], refs[-2:]
    piece = own_ref.shape[0]
    start = targets_ref.shape[1] * side
    terms = [own_ref[...]]
    for ref in reversed(arrived):
        hi = ref[start : start + piece, :].astype(F32)
        terms.append(hi + ref[start + piece :, :].astype(F32))
    piece_ref[...] = tree_sum(terms).astype(BF16)
    sums_ref[...] = part_ref[...]
    p = lax.axis_index("dom")
    for ref, k in zip(arrived, exchange_order(nd)):
        add_rows(sums_ref, ref, targets_ref, partner(p, k, nd), side)


def shard_sum_kernel(ns, side, targets_ref, part_ref, own_ref, *refs):
    arrived, pieces, (sums_ref, out_ref) = refs[: ns - 2], refs[ns - 2 : -2], refs[-2:]
    out_ref[...] = tree_sum([ref[...].astype(F32) for ref in (own_ref, *reversed(pieces))])
    sums_ref[...] = part_ref[...]
    s = lax.axis_index("shard")
    for ref, k in zip(arrived, exchange_order(ns)):
        add_rows(sums_ref, ref, targets_ref, partner(s, k, ns), side)


def finish_kernel(ns, side, targets_ref, part_ref, weight_ref, near_ref, out_ref, sums_ref):
    sums_ref[...] = part_ref[...]
    peer = partner(lax.axis_index("shard"), exchange_order(ns)[-1], ns)
    add_rows(sums_ref, near_ref, targets_ref, peer, side)
    out_ref[...] = mm3(split(sums_ref[...]), split(weight_ref[...]), ((1,), (1,)))


def place_kernel(nd, *refs):
    p = lax.axis_index("dom")
    out_ref = refs[-1]
    piece = refs[0].shape[0]
    for ref, k in zip(refs[:-1], [0] + exchange_order(nd)):
        at = pl.multiple_of(back_partner(p, k, nd) * piece, 8)
        out_ref[pl.ds(at, piece), :] = ref[...]


def on_device(features, weight, cotangent, block_values, block_list, send_inner, send_outer):
    keep = lambda x: pltpu.with_memory_space_constraint(x, pltpu.HBM)
    node_count, width = features.shape
    row_blocks, fanout, side, _ = block_values.shape
    ns = lax.axis_size("shard")
    nd = lax.axis_size("dom")
    inner_cap = send_inner.shape[2]
    outer_cap = send_outer.shape[2]
    slots = (ns - 1) * inner_cap + (nd - 1) * outer_cap
    dims = (row_blocks, fanout, side, width, ns, nd, inner_cap, outer_cap)
    shape = jax.ShapeDtypeStruct
    rows_f32 = shape((node_count, width), F32)
    rows_f16 = shape((node_count, width), BF16)
    packed_inner = [shape((inner_cap * side, width), BF16)] * (ns - 1)
    packed_outer = [shape((outer_cap * side, width), BF16)] * (nd - 1)
    nbytes = node_count * width * 4

    inner_targets = jnp.swapaxes(send_inner, 1, 2)
    outer_targets = jnp.swapaxes(send_outer, 1, 2)
    inner_table = pltpu.SMEM(inner_targets.shape, jnp.int32)
    outer_table = pltpu.SMEM(outer_targets.shape, jnp.int32)
    list_table = pltpu.SMEM(block_list.shape, jnp.int32)
    inner_order, outer_order = exchange_order(ns), exchange_order(nd)

    packed = call(
        functools.partial(pack_kernel, ns, nd, side), packed_inner + packed_outer[:-1], 0, 3 * nbytes,
        [HBM] * 3, [VMEM] * (ns - 1 + nd - 2),
        [inner_table, outer_table, pltpu.VMEM(features.shape, F32), pltpu.SemaphoreType.DMA((4,))],
    )(keep(inner_targets), keep(outer_targets), keep(features))
    inner_in = [send(x, "shard", k, ns) for x, k in zip(packed, inner_order)]
    outer_in = [send(x, "dom", k, nd) for x, k in zip(packed[ns - 1 :], outer_order)]

    near, base, local, scale, picked, turned, place = call(
        functools.partial(local_kernel, dims),
        [
            packed_outer[-1], rows_f32, rows_f32, rows_f32,
            shape((slots, side, side), BF16), shape((slots, side, side), BF16), shape((slots,), jnp.int32),
        ],
        4 * row_blocks * fanout * side * side * width * 3, 12 * nbytes,
        [HBM] * 5, [VMEM] * 6 + [SMEM],
        [
            list_table, outer_table, pltpu.VMEM(features.shape, F32), pltpu.VMEM(weight.shape, F32),
            pltpu.VMEM(block_values.shape, BF16),
            pltpu.VMEM(((row_blocks + 1) * side, 3 * width), BF16),
            pltpu.SMEM((row_blocks + ns * inner_cap + nd * outer_cap,), jnp.int32),
            pltpu.SemaphoreType.DMA((4 + row_blocks,)),
        ],
    )(keep(block_list), keep(outer_targets), keep(features), keep(weight), keep(block_values))
    outer_in.append(send(near, "dom", outer_order[-1], nd))

    n_in = ns - 1 + nd - 1
    outs = call(
        functools.partial(middle_kernel, dims),
        [rows_f32, rows_f32, rows_f16, rows_f32] + packed_inner,
        2 * slots * side * side * width * 2, 8 * nbytes,
        [SMEM] + [VMEM] * (n_in + 6), [VMEM] * (4 + ns - 1),
    )(place, *inner_in, *outer_in, base, scale, picked, turned, weight, cotangent)
    activations, scaled, half, total = outs[:4]
    inner_back = [send_back(x, "shard", k, ns) for x, k in zip(outs[4:], inner_order)]

    piece_rows = width // nd
    start = outer_cap * side
    outs = call(
        functools.partial(weight_kernel, dims, (ns - 1) * inner_cap),
        [shape((piece_rows, width), F32)] + [shape((start + 2 * piece_rows, width), BF16)] * (nd - 1),
        10 * node_count * width * width, 5 * nbytes,
        [SMEM] + [VMEM] * 6, [VMEM] * nd, [pltpu.VMEM((width, width), F32)],
    )(place, features, local, total, scaled, half, turned)
    outer_back = [send_back(x, "dom", k, nd) for x, k in zip(outs[1:], outer_order)]

    part = call(
        functools.partial(spread_kernel, dims[:4]), rows_f32,
        2 * row_blocks * fanout * side * side * width, 8 * nbytes,
        [HBM, HBM, VMEM, VMEM], VMEM,
        [
            list_table, pltpu.VMEM(block_values.shape, BF16),
            pltpu.VMEM(((row_blocks + 1) * side, width), F32), pltpu.SemaphoreType.DMA((1 + row_blocks,)),
        ],
    )(keep(block_list), keep(block_values), scaled, half)
    part, piece = call(
        functools.partial(dom_sum_kernel, nd, side), [rows_f32, shape((piece_rows, width), BF16)],
        0, 4 * nbytes, [SMEM] + [VMEM] * (nd + 1), [VMEM] * 2,
    )(outer_targets, part, outs[0], *outer_back)
    pieces = [send(piece, "shard", k, ns) for k in inner_order]
    part, weight_sum = call(
        functools.partial(shard_sum_kernel, ns, side), [rows_f32, shape((piece_rows, width), F32)],
        0, 4 * nbytes, [SMEM] + [VMEM] * (2 * ns - 1), [VMEM] * 2,
    )(inner_targets, part, piece, *inner_back[:-1], *pieces)
    gathered = [weight_sum] + [send(weight_sum, "dom", k, nd) for k in outer_order]
    grad_weight = call(
        functools.partial(place_kernel, nd), shape((width, width), F32), 0, nbytes, [VMEM] * nd, VMEM
    )(*gathered)
    grad_features = call(
        functools.partial(finish_kernel, ns, side), rows_f32, 6 * node_count * width * width, 4 * nbytes,
        [SMEM] + [VMEM] * 3, VMEM, [pltpu.VMEM((node_count, width), F32)],
    )(inner_targets, part, weight, inner_back[-1])
    return (activations, grad_features, grad_weight)


def solution(mesh):
    rows = ("copies", "shard", "dom")
    return jax.shard_map(
        on_device,
        mesh=mesh,
        in_specs=(
            P(rows, None),
            P(),
            P(rows, None),
            P(rows, None, None, None),
            P(rows, None),
            P(rows, None, None),
            P(rows, None, None),
        ),
        out_specs=(P(rows, None), P(rows, None), P("copies", None)),
        check_vma=False,
    )
```

```python
import functools
import jax
import jax.numpy as jnp
from jax import lax
from jax.experimental import pallas as pl
from jax.experimental.pallas import tpu as pltpu
from jax.sharding import PartitionSpec as P

F32 = jnp.float32
BF16 = jnp.bfloat16
VMEM = pl.BlockSpec(memory_space=pltpu.VMEM)
SMEM = pl.BlockSpec(memory_space=pltpu.SMEM)
HBM = pl.BlockSpec(memory_space=pltpu.HBM)
ANY = pl.BlockSpec(memory_space=pl.ANY)
PARAMS = pltpu.CompilerParams(vmem_limit_bytes=48 * 1024 * 1024)


def partner(i, k, n):
    if n & (n - 1) == 0:
        return i ^ k
    return (i + k) % n


def back_partner(i, k, n):
    if n & (n - 1) == 0:
        return i ^ k
    return (i + n - k) % n


def exchange_order(n):
    return sorted(range(1, n), key=lambda k: (k == 1, k))


def send(x, axis, k, n):
    return lax.ppermute(x, axis, [(i, partner(i, k, n)) for i in range(n)])


def send_back(x, axis, k, n):
    return lax.ppermute(x, axis, [(i, back_partner(i, k, n)) for i in range(n)])


def split(x):
    hi = x.astype(BF16)
    return hi, (x - hi.astype(F32)).astype(BF16)


def mm(a, b, dims=((1,), (0,))):
    return lax.dot_general(a, b, (dims, ((), ())), preferred_element_type=F32)


def mm3(a, b, dims=((1,), (0,))):
    ah, al = a
    bh, bl = b
    return mm(ah, bh, dims) + (mm(ah, bl, dims) + mm(al, bh, dims))


def call(kernel, out_shape, flops, nbytes, in_specs, out_specs, scratch=(), aliases={}):
    return pl.pallas_call(
        kernel,
        out_shape=out_shape,
        in_specs=in_specs,
        out_specs=out_specs,
        scratch_shapes=list(scratch),
        input_output_aliases=aliases,
        compiler_params=PARAMS,
        cost_estimate=pl.CostEstimate(flops=flops, bytes_accessed=nbytes, transcendentals=0),
    )


def fetch(pairs, sems):
    copies = [pltpu.make_async_copy(src, dst, sems.at[i]) for i, (src, dst) in enumerate(pairs)]
    for copy in copies:
        copy.start()
    return copies


def pack_rows(out_ref, targets_ref, peer, rows_ref, side):
    for j in range(targets_ref.shape[1]):
        target = targets_ref[0, j, peer]
        rows = rows_ref[pl.ds(pl.multiple_of(jnp.maximum(target, 0) * side, side), side), :]
        out_ref[j * side : (j + 1) * side, :] = jnp.where(target >= 0, rows, 0.0).astype(BF16)


def pack_kernel(ns, nd, side, inner_hbm, outer_hbm, features_hbm, *refs):
    out_refs, (inner_ref, outer_ref, rows_ref, sems) = refs[:-4], refs[-4:]
    half = rows_ref.shape[0] // 2
    copies = fetch(
        [
            (inner_hbm, inner_ref),
            (outer_hbm, outer_ref),
            (features_hbm.at[:half], rows_ref.at[:half]),
            (features_hbm.at[half:], rows_ref.at[half:]),
        ],
        sems,
    )
    for copy in copies:
        copy.wait()
    s = lax.axis_index("shard")
    p = lax.axis_index("dom")
    plan = [(inner_ref, partner(s, k, ns)) for k in exchange_order(ns)]
    plan += [(outer_ref, partner(p, k, nd)) for k in exchange_order(nd)[:-1]]
    for out_ref, (targets_ref, peer) in zip(out_refs, plan):
        pack_rows(out_ref, targets_ref, peer, rows_ref, side)


def slot_codes(row_blocks, ns, nd, inner_cap, outer_cap):
    s = lax.axis_index("shard")
    p = lax.axis_index("dom")
    codes = []
    for k in exchange_order(ns):
        for j in range(inner_cap):
            codes.append(row_blocks + back_partner(s, k, ns) * inner_cap + j)
    for k in exchange_order(nd):
        for j in range(outer_cap):
            codes.append(row_blocks + ns * inner_cap + back_partner(p, k, nd) * outer_cap + j)
    return codes


def local_kernel(
    dims, list_hbm, outer_hbm, features_hbm, weight_hbm, values_hbm,
    near_ref, base_ref, local_ref, scale_ref, picked_ref, turned_ref, values_ref, place_ref,
    list_ref, outer_ref, features_ref, weight_ref, sources_ref, inverse_ref, sems,
):
    row_blocks, fanout, side, width, ns, nd, inner_cap, outer_cap = dims
    pairs = [
        (list_hbm, list_ref), (outer_hbm, outer_ref), (features_hbm, features_ref), (weight_hbm, weight_ref)
    ]
    pairs += [(values_hbm.at[r], values_ref.at[r]) for r in range(row_blocks)]
    copies = fetch(pairs, sems)
    for copy in copies[:4]:
        copy.wait()
    pack_rows(near_ref, outer_ref, partner(lax.axis_index("dom"), exchange_order(nd)[-1], nd), features_ref, side)
    codes = row_blocks + ns * inner_cap + nd * outer_cap
    for c in range(codes):
        inverse_ref[c] = 0
    for n in range(row_blocks * fanout):
        inverse_ref[list_ref[n // fanout, n % fanout]] = n
    fh, fl = split(features_ref[...])
    projected = mm3((fh, fl), split(weight_ref[...]))
    sources_ref[: row_blocks * side, :width] = projected.astype(BF16)
    sources_ref[: row_blocks * side, width : 2 * width] = fh
    sources_ref[: row_blocks * side, 2 * width :] = fl
    sources_ref[row_blocks * side :, :] = jnp.zeros((side, 3 * width), BF16)
    for copy in copies[4:]:
        copy.wait()
    for r in range(row_blocks):
        rows = slice(r * side, (r + 1) * side)
        squares = jnp.zeros((side, side), F32)
        for k in range(fanout):
            block = values_ref[r, k].astype(F32)
            squares = squares + block * block
        scale = lax.rsqrt(1.0 + jnp.sum(squares, axis=1, keepdims=True))
        scale_ref[rows, :] = jnp.broadcast_to(scale, (side, width))
        total = jnp.zeros((side, 3 * width), F32)
        for k in range(0, fanout, 2):
            blocks = jnp.concatenate([values_ref[r, k], values_ref[r, k + 1]], axis=1)
            picks = []
            for kk in (k, k + 1):
                at = pl.multiple_of(jnp.minimum(list_ref[r, kk], row_blocks) * side, side)
                picks.append(sources_ref[pl.ds(at, side), :])
            total = total + mm(blocks, jnp.concatenate(picks, axis=0))
        base_ref[rows, :] = projected[rows, :] + total[:, :width]
        local_ref[rows, :] = total[:, width : 2 * width] + total[:, 2 * width :]
    for i, code in enumerate(slot_codes(row_blocks, ns, nd, inner_cap, outer_cap)):
        n = inverse_ref[code]
        r = n // fanout
        place_ref[i] = r
        block = values_ref[r, n % fanout]
        picked_ref[i] = block
        turned_ref[i] = block.T


def middle_kernel(dims, place_any, *refs):
    row_blocks, fanout, side, width, ns, nd, inner_cap, outer_cap = dims
    n_in = (ns - 1) + (nd - 1)
    arrived = refs[:n_in]
    base_ref, scale_ref, picked_ref, turned_ref, weight_ref, cotangent_ref = refs[n_in : n_in + 6]
    mixed_ref, scaled_ref, half_ref, total_ref = refs[n_in + 6 : n_in + 10]
    leaving, (place_ref, sem) = refs[n_in + 10 : -2], refs[-2:]
    copy = pltpu.make_async_copy(place_any, place_ref, sem)
    copy.start()
    terms = []
    for ref in arrived:
        for j in range(ref.shape[0] // side):
            terms.append(mm(picked_ref[len(terms)], ref[j * side : (j + 1) * side, :]))
    total_ref[...] = jnp.zeros_like(total_ref)
    copy.wait()
    for i, term in enumerate(terms):
        rows = pl.ds(pl.multiple_of(place_ref[i] * side, side), side)
        total_ref[rows, :] += term
    weight = split(weight_ref[...])
    for r in range(row_blocks):
        rows = slice(r * side, (r + 1) * side)
        scale = scale_ref[rows, :]
        mixed = (base_ref[rows, :] + mm3(split(total_ref[rows, :]), weight)) * scale
        gate = jax.nn.sigmoid(mixed)
        mixed_ref[rows, :] = mixed
        scaled = cotangent_ref[rows, :] * gate * (1.0 + mixed * (1.0 - gate)) * scale
        scaled_ref[rows, :] = scaled
        half_ref[rows, :] = scaled.astype(BF16)
    i = 0
    for ref in leaving:
        for j in range(inner_cap):
            rows = pl.ds(pl.multiple_of(place_ref[i] * side, side), side)
            ref[j * side : (j + 1) * side, :] = mm(turned_ref[i], half_ref[rows, :]).astype(BF16)
            i += 1


def turn_rows(ref, place_ref, turned_ref, half_ref, first, count, side):
    for j in range(count):
        rows = pl.ds(pl.multiple_of(place_ref[first + j] * side, side), side)
        ref[j * side : (j + 1) * side, :] = mm(turned_ref[first + j], half_ref[rows, :]).astype(BF16)


def weight_kernel(
    dims, first, place_any, features_ref, local_ref, total_ref, scaled_ref, half_ref, turned_ref, own_ref, *refs
):
    row_blocks, fanout, side, width, ns, nd, inner_cap, outer_cap = dims
    leaving, (term_ref, place_ref, sem) = refs[:-3], refs[-3:]
    copy = pltpu.make_async_copy(place_any, place_ref, sem)
    copy.start()
    down = ((0,), (0,))
    ah, al = split(local_ref[...] + total_ref[...])
    half = half_ref[...]
    term = mm3(split(features_ref[...]), split(scaled_ref[...]), down)
    term_ref[...] = term + (mm(ah, half, down) + mm(al, half, down))
    count = own_ref.shape[0]
    mine = lax.axis_index("dom") & 1
    own_ref[...] = term_ref[pl.ds(pl.multiple_of(mine * count, 8), count), :]
    hi, lo = split(term_ref[pl.ds(pl.multiple_of((1 - mine) * count, 8), count), :])
    copy.wait()
    for i, ref in enumerate(leaving):
        turn_rows(ref, place_ref, turned_ref, half_ref, first + i * outer_cap, outer_cap, side)
    start = outer_cap * side
    leaving[-1][start : start + count, :] = hi
    leaving[-1][start + count :, :] = lo


def halve(rows, bit, own_ref, give_ref, total_ref):
    mine = (lax.axis_index("dom") >> bit) & 1
    own_ref[...] = total_ref[pl.ds(pl.multiple_of(mine * rows, 8), rows), :]
    give_ref[...] = total_ref[pl.ds(pl.multiple_of((1 - mine) * rows, 8), rows), :]


def near_sum_kernel(start, own_ref, load_ref, next_ref, give_ref, total_ref):
    count = own_ref.shape[0]
    hi = load_ref[start : start + count, :].astype(F32)
    total_ref[...] = own_ref[...] + (hi + load_ref[start + count :, :].astype(F32))
    halve(next_ref.shape[0], 1, next_ref, give_ref, total_ref)


def far_sum_kernel(bit, own_ref, load_ref, next_ref, give_ref, total_ref):
    total_ref[...] = own_ref[...] + load_ref[...]
    halve(next_ref.shape[0], bit, next_ref, give_ref, total_ref)


def last_sum_kernel(own_ref, load_ref, *refs):
    refs[-1][...] = (own_ref[...] + load_ref[...]).astype(BF16)


def shard_sum_kernel(ns, own_ref, *refs):
    terms = dict(zip([0] + exchange_order(ns), (own_ref, *refs)))
    refs[-1][...] = tree_sum([terms[k][...].astype(F32) for k in range(ns)])


def join_kernel(bit, own_ref, load_ref, *refs):
    rows = own_ref.shape[0]
    mine = (lax.axis_index("dom") >> bit) & 1
    refs[-1][pl.ds(pl.multiple_of(mine * rows, 8), rows), :] = own_ref[...]
    refs[-1][pl.ds(pl.multiple_of((1 - mine) * rows, 8), rows), :] = load_ref[...]


def spread_kernel(
    dims, list_any, values_ref, mixed_ref, scaled_ref, half_ref, act_hbm, out_ref, act_ref, list_ref, sums_ref, sems
):
    row_blocks, fanout, side, width = dims
    (listed,) = fetch([(list_any, list_ref)], sems)
    mixed = mixed_ref[...]
    act_ref[...] = mixed * jax.nn.sigmoid(mixed)
    store = pltpu.make_async_copy(act_ref, act_hbm, sems.at[1])
    store.start()
    sums_ref[...] = jnp.zeros_like(sums_ref)
    listed.wait()
    for r in range(row_blocks):
        half = half_ref[r * side : (r + 1) * side, :].astype(F32).T.astype(BF16)
        for k in range(0, fanout, 2):
            blocks = jnp.concatenate([values_ref[r, k], values_ref[r, k + 1]], axis=1)
            terms = mm(half, blocks)
            for kk in (0, 1):
                sums_ref[jnp.minimum(list_ref[r, k + kk], row_blocks)] += terms[:, kk * side : (kk + 1) * side]
    for c in range(row_blocks):
        rows = slice(c * side, (c + 1) * side)
        out_ref[rows, :] = scaled_ref[rows, :] + sums_ref[c].T
    store.wait()


def tree_sum(terms):
    while len(terms) > 1:
        terms = [sum(terms[i : i + 2][1:], terms[i]) for i in range(0, len(terms), 2)]
    return terms[0]


def add_rows(sums_ref, ref, targets_ref, peer, side):
    for j in range(targets_ref.shape[1]):
        target = targets_ref[0, j, peer]
        rows = pl.ds(pl.multiple_of(jnp.maximum(target, 0) * side, side), side)
        term = ref[j * side : (j + 1) * side, :].astype(F32)
        sums_ref[rows, :] += jnp.where(target >= 0, term, 0.0)


def finish_kernel(items, sizes, side, inner_any, outer_any, part_ref, weight_ref, *refs):
    arrived, (out_hbm, out_ref, sums_ref, inner_ref, outer_ref, sems) = refs[:-6], refs[-6:]
    tables = fetch([(inner_any, inner_ref), (outer_any, outer_ref)], sems)
    sums_ref[...] = part_ref[...]
    weight = split(weight_ref[...])
    for copy in tables:
        copy.wait()
    for (axis, k), ref in zip(items, arrived):
        targets_ref = inner_ref if axis == "shard" else outer_ref
        add_rows(sums_ref, ref, targets_ref, partner(lax.axis_index(axis), k, sizes[axis]), side)
    stores = []
    for r in range(sums_ref.shape[0] // side):
        rows = slice(r * side, (r + 1) * side)
        out_ref[rows, :] = mm3(split(sums_ref[rows, :]), weight, ((1,), (1,)))
        stores.append(pltpu.make_async_copy(out_ref.at[rows], out_hbm.at[rows], sems.at[2 + r]))
        stores[-1].start()
    for store in stores:
        store.wait()


GATES = {"last": [("dom", 2), ("dom", 3), ("dom", 1)], "shard": [("shard", 2)], "join": [("shard", 3), ("shard", 1)], "place": []}


def on_device(features, weight, cotangent, block_values, block_list, send_inner, send_outer):
    keep = lambda x: pltpu.with_memory_space_constraint(x, pltpu.HBM)
    node_count, width = features.shape
    row_blocks, fanout, side, _ = block_values.shape
    ns = lax.axis_size("shard")
    nd = lax.axis_size("dom")
    inner_cap = send_inner.shape[2]
    outer_cap = send_outer.shape[2]
    slots = (ns - 1) * inner_cap + (nd - 1) * outer_cap
    dims = (row_blocks, fanout, side, width, ns, nd, inner_cap, outer_cap)
    shape = jax.ShapeDtypeStruct
    rows_f32 = shape((node_count, width), F32)
    rows_f16 = shape((node_count, width), BF16)
    packed_inner = [shape((inner_cap * side, width), BF16)] * (ns - 1)
    packed_outer = [shape((outer_cap * side, width), BF16)] * (nd - 1)
    nbytes = node_count * width * 4

    inner_targets = jnp.swapaxes(send_inner, 1, 2)
    outer_targets = jnp.swapaxes(send_outer, 1, 2)
    inner_table = pltpu.SMEM(inner_targets.shape, jnp.int32)
    outer_table = pltpu.SMEM(outer_targets.shape, jnp.int32)
    list_table = pltpu.SMEM(block_list.shape, jnp.int32)
    inner_order, outer_order = exchange_order(ns), exchange_order(nd)

    packed = call(
        functools.partial(pack_kernel, ns, nd, side), packed_inner + packed_outer[:-1], 0, 3 * nbytes,
        [HBM] * 3, [VMEM] * (ns - 1 + nd - 2),
        [inner_table, outer_table, pltpu.VMEM(features.shape, F32), pltpu.SemaphoreType.DMA((4,))],
    )(keep(inner_targets), keep(outer_targets), keep(features))
    inner_in = [send(x, "shard", k, ns) for x, k in zip(packed, inner_order)]
    outer_in = [send(x, "dom", k, nd) for x, k in zip(packed[ns - 1 :], outer_order)]

    near, base, local, scale, picked, turned, values, place = call(
        functools.partial(local_kernel, dims),
        [
            packed_outer[-1], rows_f32, rows_f32, rows_f32,
            shape((slots, side, side), BF16), shape((slots, side, side), BF16),
            shape(block_values.shape, BF16), shape((slots,), jnp.int32),
        ],
        4 * row_blocks * fanout * side * side * width * 3, 12 * nbytes,
        [HBM] * 5, [VMEM] * 7 + [SMEM],
        [
            list_table, outer_table, pltpu.VMEM(features.shape, F32), pltpu.VMEM(weight.shape, F32),
            pltpu.VMEM(((row_blocks + 1) * side, 3 * width), BF16),
            pltpu.SMEM((row_blocks + ns * inner_cap + nd * outer_cap,), jnp.int32),
            pltpu.SemaphoreType.DMA((4 + row_blocks,)),
        ],
    )(keep(block_list), keep(outer_targets), keep(features), keep(weight), keep(block_values))
    outer_in.append(send(near, "dom", outer_order[-1], nd))

    n_in = ns - 1 + nd - 1
    outs = call(
        functools.partial(middle_kernel, dims),
        [rows_f32, rows_f32, rows_f16, rows_f32] + packed_inner,
        2 * slots * side * side * width * 2, 8 * nbytes,
        [ANY] + [VMEM] * (n_in + 6), [VMEM] * (4 + ns - 1),
        [pltpu.SMEM((slots,), jnp.int32), pltpu.SemaphoreType.DMA],
    )(place, *inner_in, *outer_in, base, scale, picked, turned, weight, cotangent)
    mixed, scaled, half, total = outs[:4]
    inner_back = [send_back(x, "shard", k, ns) for x, k in zip(outs[4:], inner_order)]

    count = width // 2
    outs = call(
        functools.partial(weight_kernel, dims, (ns - 1) * inner_cap),
        [shape((count, width), F32)] + packed_outer[:-1] + [shape((outer_cap * side + 2 * count, width), BF16)],
        10 * node_count * width * width, 5 * nbytes,
        [ANY] + [VMEM] * 6, [VMEM] * nd,
        [pltpu.VMEM((width, width), F32), pltpu.SMEM((slots,), jnp.int32), pltpu.SemaphoreType.DMA],
    )(place, features, local, total, scaled, half, turned)
    own, outer_terms = outs[0], outs[1:]
    near_back = send_back(outer_terms[-1], "dom", 1, nd)
    outer_back = [send_back(x, "dom", k, nd) for x, k in zip(outer_terms[:-1], outer_order)] + [near_back]

    activations, part = call(
        functools.partial(spread_kernel, dims[:4]), [rows_f32, rows_f32],
        2 * row_blocks * fanout * side * side * width, 8 * nbytes,
        [ANY] + [VMEM] * 4, [HBM, VMEM],
        [
            pltpu.VMEM((node_count, width), F32), list_table, pltpu.VMEM((row_blocks + 1, width, side), F32),
            pltpu.SemaphoreType.DMA((2,)),
        ],
    )(block_list, values, mixed, scaled, half)

    back = {("shard", k): x for k, x in zip(inner_order, inner_back)}
    back.update({("dom", k): x for k, x in zip(outer_order, outer_back)})
    sizes = {"shard": ns, "dom": nd}

    def stage(kernel, name, inputs, rows, dtype=F32):
        gated = [back[item] for item in GATES[name] if item in back] + [part] * (name == "shard")
        return call(
            kernel, shape((rows, width), dtype), 0, nbytes // 4,
            [VMEM] * len(inputs) + [ANY] * len(gated), VMEM,
        )(*inputs, *gated)

    bits = nd.bit_length() - 1
    load = near_back
    for bit in range(bits):
        if bit == bits - 1:
            piece = stage(last_sum_kernel, "last", [own, load], count, BF16)
            break
        kernel = functools.partial(near_sum_kernel, outer_cap * side) if bit == 0 else functools.partial(far_sum_kernel, bit + 1)
        count //= 2
        own, give = call(
            kernel, [shape((count, width), F32)] * 2, 0, nbytes // 4,
            [VMEM] * 2, [VMEM] * 2, [pltpu.VMEM((2 * count, width), F32)],
        )(own, load)
        load = send(give, "dom", 2 << bit, nd)
    pieces = [piece] + [send(piece, "shard", k, ns) for k in inner_order]
    weight_sum = stage(functools.partial(shard_sum_kernel, ns), "shard", pieces, count)
    for bit in reversed(range(bits)):
        count *= 2
        load = send(weight_sum, "dom", 1 << bit, nd)
        weight_sum = stage(
            functools.partial(join_kernel, bit), "join" if bit == 1 else "place", [weight_sum, load], count
        )
    grad_features = call(
        functools.partial(finish_kernel, list(back), sizes, side), rows_f32,
        6 * node_count * width * width, 4 * nbytes, [ANY] * 2 + [VMEM] * (2 + len(back)), HBM,
        [
            pltpu.VMEM((node_count, width), F32), pltpu.VMEM((node_count, width), F32), inner_table, outer_table,
            pltpu.SemaphoreType.DMA((2 + row_blocks,)),
        ],
    )(inner_targets, outer_targets, part, weight, *back.values())
    grad_weight = weight_sum
    return (activations, grad_features, grad_weight)


def solution(mesh):
    rows = ("copies", "shard", "dom")
    return jax.shard_map(
        on_device,
        mesh=mesh,
        in_specs=(
            P(rows, None),
            P(),
            P(rows, None),
            P(rows, None, None, None),
            P(rows, None),
            P(rows, None, None),
            P(rows, None, None),
        ),
        out_specs=(P(rows, None), P(rows, None), P("copies", None)),
        check_vma=False,
    )
```

```python
import functools
import jax
import jax.numpy as jnp
from jax import lax
from jax.experimental import pallas as pl
from jax.experimental.pallas import tpu as pltpu
from jax.sharding import PartitionSpec as P

F32 = jnp.float32
BF16 = jnp.bfloat16
VMEM = pl.BlockSpec(memory_space=pltpu.VMEM)
SMEM = pl.BlockSpec(memory_space=pltpu.SMEM)
HBM = pl.BlockSpec(memory_space=pltpu.HBM)
ANY = pl.BlockSpec(memory_space=pl.ANY)
PARAMS = pltpu.CompilerParams(vmem_limit_bytes=48 * 1024 * 1024)


def partner(i, k, n):
    if n & (n - 1) == 0:
        return i ^ k
    return (i + k) % n


def back_partner(i, k, n):
    if n & (n - 1) == 0:
        return i ^ k
    return (i + n - k) % n


def exchange_order(n):
    return sorted(range(1, n), key=lambda k: (k == 1, k))


def send(x, axis, k, n):
    return lax.ppermute(x, axis, [(i, partner(i, k, n)) for i in range(n)])


def send_back(x, axis, k, n):
    return lax.ppermute(x, axis, [(i, back_partner(i, k, n)) for i in range(n)])


def split(x):
    hi = x.astype(BF16)
    return hi, (x - hi.astype(F32)).astype(BF16)


def mm(a, b, dims=((1,), (0,))):
    return lax.dot_general(a, b, (dims, ((), ())), preferred_element_type=F32)


def mm3(a, b, dims=((1,), (0,))):
    ah, al = a
    bh, bl = b
    return mm(ah, bh, dims) + (mm(ah, bl, dims) + mm(al, bh, dims))


def call(kernel, out_shape, flops, nbytes, in_specs, out_specs, scratch=(), aliases={}):
    return pl.pallas_call(
        kernel,
        out_shape=out_shape,
        in_specs=in_specs,
        out_specs=out_specs,
        scratch_shapes=list(scratch),
        input_output_aliases=aliases,
        compiler_params=PARAMS,
        cost_estimate=pl.CostEstimate(flops=flops, bytes_accessed=nbytes, transcendentals=0),
    )


def fetch(pairs, sems):
    copies = [pltpu.make_async_copy(src, dst, sems.at[i]) for i, (src, dst) in enumerate(pairs)]
    for copy in copies:
        copy.start()
    return copies


def pack_rows(out_ref, targets_ref, peer, rows_ref, side):
    for j in range(targets_ref.shape[1]):
        target = targets_ref[0, j, peer]
        rows = rows_ref[pl.ds(pl.multiple_of(jnp.maximum(target, 0) * side, side), side), :]
        out_ref[j * side : (j + 1) * side, :] = jnp.where(target >= 0, rows, 0.0).astype(BF16)


def pack_kernel(ns, nd, side, inner_hbm, outer_hbm, features_hbm, *refs):
    out_refs, (inner_ref, outer_ref, rows_ref, sems) = refs[:-4], refs[-4:]
    half = rows_ref.shape[0] // 2
    copies = fetch(
        [
            (inner_hbm, inner_ref),
            (outer_hbm, outer_ref),
            (features_hbm.at[:half], rows_ref.at[:half]),
            (features_hbm.at[half:], rows_ref.at[half:]),
        ],
        sems,
    )
    for copy in copies:
        copy.wait()
    s = lax.axis_index("shard")
    p = lax.axis_index("dom")
    plan = [(inner_ref, partner(s, k, ns)) for k in exchange_order(ns)]
    plan += [(outer_ref, partner(p, k, nd)) for k in exchange_order(nd)[:-1]]
    for out_ref, (targets_ref, peer) in zip(out_refs, plan):
        pack_rows(out_ref, targets_ref, peer, rows_ref, side)


def slot_codes(row_blocks, ns, nd, inner_cap, outer_cap):
    s = lax.axis_index("shard")
    p = lax.axis_index("dom")
    codes = []
    for k in exchange_order(ns):
        for j in range(inner_cap):
            codes.append(row_blocks + back_partner(s, k, ns) * inner_cap + j)
    for k in exchange_order(nd):
        for j in range(outer_cap):
            codes.append(row_blocks + ns * inner_cap + back_partner(p, k, nd) * outer_cap + j)
    return codes


def local_kernel(
    dims, list_hbm, outer_hbm, features_hbm, weight_hbm, values_hbm,
    near_ref, base_ref, local_ref, scale_ref, picked_ref, turned_ref, values_ref, place_ref,
    list_ref, outer_ref, features_ref, weight_ref, sources_ref, inverse_ref, sems,
):
    row_blocks, fanout, side, width, ns, nd, inner_cap, outer_cap = dims
    pairs = [
        (list_hbm, list_ref), (outer_hbm, outer_ref), (features_hbm, features_ref), (weight_hbm, weight_ref)
    ]
    pairs += [(values_hbm.at[r], values_ref.at[r]) for r in range(row_blocks)]
    copies = fetch(pairs, sems)
    for copy in copies[:4]:
        copy.wait()
    pack_rows(near_ref, outer_ref, partner(lax.axis_index("dom"), exchange_order(nd)[-1], nd), features_ref, side)
    codes = row_blocks + ns * inner_cap + nd * outer_cap
    for c in range(codes):
        inverse_ref[c] = 0
    for n in range(row_blocks * fanout):
        inverse_ref[list_ref[n // fanout, n % fanout]] = n
    fh, fl = split(features_ref[...])
    projected = mm3((fh, fl), split(weight_ref[...]))
    sources_ref[: row_blocks * side, :width] = projected.astype(BF16)
    sources_ref[: row_blocks * side, width : 2 * width] = fh
    sources_ref[: row_blocks * side, 2 * width :] = fl
    sources_ref[row_blocks * side :, :] = jnp.zeros((side, 3 * width), BF16)
    for copy in copies[4:]:
        copy.wait()
    for r in range(row_blocks):
        rows = slice(r * side, (r + 1) * side)
        squares = jnp.zeros((side, side), F32)
        for k in range(fanout):
            block = values_ref[r, k].astype(F32)
            squares = squares + block * block
        scale = lax.rsqrt(1.0 + jnp.sum(squares, axis=1, keepdims=True))
        scale_ref[rows, :] = jnp.broadcast_to(scale, (side, width))
        total = jnp.zeros((side, 3 * width), F32)
        for k in range(0, fanout, 2):
            blocks = jnp.concatenate([values_ref[r, k], values_ref[r, k + 1]], axis=1)
            picks = []
            for kk in (k, k + 1):
                at = pl.multiple_of(jnp.minimum(list_ref[r, kk], row_blocks) * side, side)
                picks.append(sources_ref[pl.ds(at, side), :])
            total = total + mm(blocks, jnp.concatenate(picks, axis=0))
        base_ref[rows, :] = projected[rows, :] + total[:, :width]
        local_ref[rows, :] = total[:, width : 2 * width] + total[:, 2 * width :]
    for i, code in enumerate(slot_codes(row_blocks, ns, nd, inner_cap, outer_cap)):
        n = inverse_ref[code]
        r = n // fanout
        place_ref[i] = r
        block = values_ref[r, n % fanout]
        picked_ref[i] = block
        turned_ref[i] = block.T


def middle_kernel(dims, place_any, *refs):
    row_blocks, fanout, side, width, ns, nd, inner_cap, outer_cap = dims
    n_in = (ns - 1) + (nd - 1)
    arrived = refs[:n_in]
    base_ref, scale_ref, picked_ref, turned_ref, weight_ref, cotangent_ref = refs[n_in : n_in + 6]
    mixed_ref, scaled_ref, half_ref, total_ref = refs[n_in + 6 : n_in + 10]
    leaving, (place_ref, sem) = refs[n_in + 10 : -2], refs[-2:]
    copy = pltpu.make_async_copy(place_any, place_ref, sem)
    copy.start()
    terms = []
    for ref in arrived:
        for j in range(ref.shape[0] // side):
            terms.append(mm(picked_ref[len(terms)], ref[j * side : (j + 1) * side, :]))
    total_ref[...] = jnp.zeros_like(total_ref)
    copy.wait()
    for i, term in enumerate(terms):
        rows = pl.ds(pl.multiple_of(place_ref[i] * side, side), side)
        total_ref[rows, :] += term
    weight = split(weight_ref[...])
    for r in range(row_blocks):
        rows = slice(r * side, (r + 1) * side)
        scale = scale_ref[rows, :]
        mixed = (base_ref[rows, :] + mm3(split(total_ref[rows, :]), weight)) * scale
        gate = jax.nn.sigmoid(mixed)
        mixed_ref[rows, :] = mixed
        scaled = cotangent_ref[rows, :] * gate * (1.0 + mixed * (1.0 - gate)) * scale
        scaled_ref[rows, :] = scaled
        half_ref[rows, :] = scaled.astype(BF16)
    i = 0
    for ref in leaving:
        for j in range(inner_cap):
            rows = pl.ds(pl.multiple_of(place_ref[i] * side, side), side)
            ref[j * side : (j + 1) * side, :] = mm(turned_ref[i], half_ref[rows, :]).astype(BF16)
            i += 1


def turn_rows(ref, place_ref, turned_ref, half_ref, first, count, side):
    for j in range(count):
        rows = pl.ds(pl.multiple_of(place_ref[first + j] * side, side), side)
        ref[j * side : (j + 1) * side, :] = mm(turned_ref[first + j], half_ref[rows, :]).astype(BF16)


def weight_kernel(
    dims, first, place_any, features_ref, local_ref, total_ref, scaled_ref, half_ref, turned_ref, own_ref, *refs
):
    row_blocks, fanout, side, width, ns, nd, inner_cap, outer_cap = dims
    leaving, (term_ref, place_ref, sem) = refs[:-3], refs[-3:]
    copy = pltpu.make_async_copy(place_any, place_ref, sem)
    copy.start()
    down = ((0,), (0,))
    ah, al = split(local_ref[...] + total_ref[...])
    half = half_ref[...]
    term = mm3(split(features_ref[...]), split(scaled_ref[...]), down)
    term_ref[...] = term + (mm(ah, half, down) + mm(al, half, down))
    count = own_ref.shape[0]
    mine = lax.axis_index("dom") & 1
    own_ref[...] = term_ref[pl.ds(pl.multiple_of(mine * count, 8), count), :]
    hi, lo = split(term_ref[pl.ds(pl.multiple_of((1 - mine) * count, 8), count), :])
    copy.wait()
    for i, ref in enumerate(leaving):
        turn_rows(ref, place_ref, turned_ref, half_ref, first + i * outer_cap, outer_cap, side)
    start = outer_cap * side
    leaving[-1][start : start + count, :] = hi
    leaving[-1][start + count :, :] = lo


def halve(rows, bit, own_ref, give_ref, total_ref):
    mine = (lax.axis_index("dom") >> bit) & 1
    own_ref[...] = total_ref[pl.ds(pl.multiple_of(mine * rows, 8), rows), :]
    give_ref[...] = total_ref[pl.ds(pl.multiple_of((1 - mine) * rows, 8), rows), :]


def near_sum_kernel(start, own_ref, load_ref, next_ref, give_ref, total_ref):
    count = own_ref.shape[0]
    hi = load_ref[start : start + count, :].astype(F32)
    total_ref[...] = own_ref[...] + (hi + load_ref[start + count :, :].astype(F32))
    halve(next_ref.shape[0], 1, next_ref, give_ref, total_ref)


def far_sum_kernel(bit, own_ref, load_ref, next_ref, give_ref, total_ref):
    total_ref[...] = own_ref[...] + load_ref[...]
    halve(next_ref.shape[0], bit, next_ref, give_ref, total_ref)


def last_sum_kernel(own_ref, load_ref, *refs):
    refs[-1][...] = (own_ref[...] + load_ref[...]).astype(BF16)


def shard_sum_kernel(ns, own_ref, *refs):
    terms = dict(zip([0] + exchange_order(ns), (own_ref, *refs)))
    refs[-1][...] = tree_sum([terms[k][...].astype(F32) for k in range(ns)])


def owned_piece(index, nd):
    bits = nd.bit_length() - 1
    return sum(((index >> bit) & 1) << (bits - 1 - bit) for bit in range(bits))


def place_kernel(nd, *refs):
    p = lax.axis_index("dom")
    rows = refs[0].shape[0]
    for ref, k in zip(refs, [0] + exchange_order(nd)):
        at = pl.multiple_of(owned_piece(partner(p, k, nd), nd) * rows, 8)
        refs[-1][pl.ds(at, rows), :] = ref[...]


def spread_kernel(
    dims, list_any, values_ref, mixed_ref, scaled_ref, half_ref, act_hbm, out_ref, act_ref, list_ref, sums_ref, sems
):
    row_blocks, fanout, side, width = dims
    (listed,) = fetch([(list_any, list_ref)], sems)
    mixed = mixed_ref[...]
    act_ref[...] = mixed * jax.nn.sigmoid(mixed)
    store = pltpu.make_async_copy(act_ref, act_hbm, sems.at[1])
    store.start()
    sums_ref[...] = jnp.zeros_like(sums_ref)
    listed.wait()
    for r in range(row_blocks):
        half = half_ref[r * side : (r + 1) * side, :].astype(F32).T.astype(BF16)
        for k in range(0, fanout, 2):
            blocks = jnp.concatenate([values_ref[r, k], values_ref[r, k + 1]], axis=1)
            terms = mm(half, blocks)
            for kk in (0, 1):
                sums_ref[jnp.minimum(list_ref[r, k + kk], row_blocks)] += terms[:, kk * side : (kk + 1) * side]
    for c in range(row_blocks):
        rows = slice(c * side, (c + 1) * side)
        out_ref[rows, :] = scaled_ref[rows, :] + sums_ref[c].T
    store.wait()


def tree_sum(terms):
    while len(terms) > 1:
        terms = [sum(terms[i : i + 2][1:], terms[i]) for i in range(0, len(terms), 2)]
    return terms[0]


def add_rows(sums_ref, ref, targets_ref, peer, side):
    for j in range(targets_ref.shape[1]):
        target = targets_ref[0, j, peer]
        rows = pl.ds(pl.multiple_of(jnp.maximum(target, 0) * side, side), side)
        term = ref[j * side : (j + 1) * side, :].astype(F32)
        sums_ref[rows, :] += jnp.where(target >= 0, term, 0.0)


def finish_kernel(items, sizes, side, inner_any, outer_any, part_ref, weight_ref, *refs):
    arrived, (out_hbm, out_ref, sums_ref, inner_ref, outer_ref, sems) = refs[:-6], refs[-6:]
    tables = fetch([(inner_any, inner_ref), (outer_any, outer_ref)], sems)
    sums_ref[...] = part_ref[...]
    weight = split(weight_ref[...])
    for copy in tables:
        copy.wait()
    for (axis, k), ref in zip(items, arrived):
        targets_ref = inner_ref if axis == "shard" else outer_ref
        add_rows(sums_ref, ref, targets_ref, partner(lax.axis_index(axis), k, sizes[axis]), side)
    stores = []
    for r in range(sums_ref.shape[0] // side):
        rows = slice(r * side, (r + 1) * side)
        out_ref[rows, :] = mm3(split(sums_ref[rows, :]), weight, ((1,), (1,)))
        stores.append(pltpu.make_async_copy(out_ref.at[rows], out_hbm.at[rows], sems.at[2 + r]))
        stores[-1].start()
    for store in stores:
        store.wait()


GATES = {"last": [("dom", 1), ("dom", 2), ("dom", 3)], "shard": ["part", ("shard", 2), ("shard", 3), ("shard", 1)], "place": ["finish"]}


def on_device(features, weight, cotangent, block_values, block_list, send_inner, send_outer):
    keep = lambda x: pltpu.with_memory_space_constraint(x, pltpu.HBM)
    node_count, width = features.shape
    row_blocks, fanout, side, _ = block_values.shape
    ns = lax.axis_size("shard")
    nd = lax.axis_size("dom")
    inner_cap = send_inner.shape[2]
    outer_cap = send_outer.shape[2]
    slots = (ns - 1) * inner_cap + (nd - 1) * outer_cap
    dims = (row_blocks, fanout, side, width, ns, nd, inner_cap, outer_cap)
    shape = jax.ShapeDtypeStruct
    rows_f32 = shape((node_count, width), F32)
    rows_f16 = shape((node_count, width), BF16)
    packed_inner = [shape((inner_cap * side, width), BF16)] * (ns - 1)
    packed_outer = [shape((outer_cap * side, width), BF16)] * (nd - 1)
    nbytes = node_count * width * 4

    inner_targets = jnp.swapaxes(send_inner, 1, 2)
    outer_targets = jnp.swapaxes(send_outer, 1, 2)
    inner_table = pltpu.SMEM(inner_targets.shape, jnp.int32)
    outer_table = pltpu.SMEM(outer_targets.shape, jnp.int32)
    list_table = pltpu.SMEM(block_list.shape, jnp.int32)
    inner_order, outer_order = exchange_order(ns), exchange_order(nd)

    packed = call(
        functools.partial(pack_kernel, ns, nd, side), packed_inner + packed_outer[:-1], 0, 3 * nbytes,
        [HBM] * 3, [VMEM] * (ns - 1 + nd - 2),
        [inner_table, outer_table, pltpu.VMEM(features.shape, F32), pltpu.SemaphoreType.DMA((4,))],
    )(keep(inner_targets), keep(outer_targets), keep(features))
    inner_in = [send(x, "shard", k, ns) for x, k in zip(packed, inner_order)]
    outer_in = [send(x, "dom", k, nd) for x, k in zip(packed[ns - 1 :], outer_order)]

    near, base, local, scale, picked, turned, values, place = call(
        functools.partial(local_kernel, dims),
        [
            packed_outer[-1], rows_f32, rows_f32, rows_f32,
            shape((slots, side, side), BF16), shape((slots, side, side), BF16),
            shape(block_values.shape, BF16), shape((slots,), jnp.int32),
        ],
        4 * row_blocks * fanout * side * side * width * 3, 12 * nbytes,
        [HBM] * 5, [VMEM] * 7 + [SMEM],
        [
            list_table, outer_table, pltpu.VMEM(features.shape, F32), pltpu.VMEM(weight.shape, F32),
            pltpu.VMEM(((row_blocks + 1) * side, 3 * width), BF16),
            pltpu.SMEM((row_blocks + ns * inner_cap + nd * outer_cap,), jnp.int32),
            pltpu.SemaphoreType.DMA((4 + row_blocks,)),
        ],
    )(keep(block_list), keep(outer_targets), keep(features), keep(weight), keep(block_values))
    outer_in.append(send(near, "dom", outer_order[-1], nd))

    n_in = ns - 1 + nd - 1
    outs = call(
        functools.partial(middle_kernel, dims),
        [rows_f32, rows_f32, rows_f16, rows_f32] + packed_inner,
        2 * slots * side * side * width * 2, 8 * nbytes,
        [ANY] + [VMEM] * (n_in + 6), [VMEM] * (4 + ns - 1),
        [pltpu.SMEM((slots,), jnp.int32), pltpu.SemaphoreType.DMA],
    )(place, *inner_in, *outer_in, base, scale, picked, turned, weight, cotangent)
    mixed, scaled, half, total = outs[:4]
    inner_back = [send_back(x, "shard", k, ns) for x, k in zip(outs[4:], inner_order)]

    count = width // 2
    outs = call(
        functools.partial(weight_kernel, dims, (ns - 1) * inner_cap),
        [shape((count, width), F32)] + packed_outer[:-1] + [shape((outer_cap * side + 2 * count, width), BF16)],
        10 * node_count * width * width, 5 * nbytes,
        [ANY] + [VMEM] * 6, [VMEM] * nd,
        [pltpu.VMEM((width, width), F32), pltpu.SMEM((slots,), jnp.int32), pltpu.SemaphoreType.DMA],
    )(place, features, local, total, scaled, half, turned)
    own, outer_terms = outs[0], outs[1:]
    near_back = send_back(outer_terms[-1], "dom", 1, nd)
    outer_back = [send_back(x, "dom", k, nd) for x, k in zip(outer_terms[:-1], outer_order)] + [near_back]

    activations, part = call(
        functools.partial(spread_kernel, dims[:4]), [rows_f32, rows_f32],
        2 * row_blocks * fanout * side * side * width, 8 * nbytes,
        [ANY] + [VMEM] * 4, [HBM, VMEM],
        [
            pltpu.VMEM((node_count, width), F32), list_table, pltpu.VMEM((row_blocks + 1, width, side), F32),
            pltpu.SemaphoreType.DMA((2,)),
        ],
    )(block_list, values, mixed, scaled, half)

    back = {("shard", k): x for k, x in zip(inner_order, inner_back)}
    back.update({("dom", k): x for k, x in zip(outer_order, outer_back)})
    sizes = {"shard": ns, "dom": nd}

    grad_features = call(
        functools.partial(finish_kernel, list(back), sizes, side), rows_f32,
        6 * node_count * width * width, 4 * nbytes, [ANY] * 2 + [VMEM] * (2 + len(back)), HBM,
        [
            pltpu.VMEM((node_count, width), F32), pltpu.VMEM((node_count, width), F32), inner_table, outer_table,
            pltpu.SemaphoreType.DMA((2 + row_blocks,)),
        ],
    )(inner_targets, outer_targets, part, weight, *back.values())
    back["part"] = part
    back["finish"] = keep(grad_features)

    def stage(kernel, name, inputs, rows, dtype=F32):
        gated = [back[item] for item in GATES.get(name, ()) if item in back]
        return call(
            kernel, shape((rows, width), dtype), 0, nbytes // 4,
            [VMEM] * len(inputs) + [ANY] * len(gated), VMEM,
        )(*inputs, *gated)

    bits = nd.bit_length() - 1
    load = near_back
    for bit in range(bits):
        if bit == bits - 1:
            piece = stage(last_sum_kernel, "last", [own, load], count, BF16)
            break
        kernel = functools.partial(near_sum_kernel, outer_cap * side) if bit == 0 else functools.partial(far_sum_kernel, bit + 1)
        count //= 2
        own, give = call(
            kernel, [shape((count, width), F32)] * 2, 0, nbytes // 4,
            [VMEM] * 2, [VMEM] * 2, [pltpu.VMEM((2 * count, width), F32)],
        )(own, load)
        load = send(give, "dom", 2 << bit, nd)
    pieces = [piece] + [send(piece, "shard", k, ns) for k in inner_order]
    weight_sum = stage(functools.partial(shard_sum_kernel, ns), "shard", pieces, count)
    pieces = [weight_sum] + [send(weight_sum, "dom", k, nd) for k in outer_order]
    weight_sum = stage(functools.partial(place_kernel, nd), "place", pieces, width)
    grad_weight = weight_sum
    return (activations, grad_features, grad_weight)


def solution(mesh):
    rows = ("copies", "shard", "dom")
    return jax.shard_map(
        on_device,
        mesh=mesh,
        in_specs=(
            P(rows, None),
            P(),
            P(rows, None),
            P(rows, None, None, None),
            P(rows, None),
            P(rows, None, None),
            P(rows, None, None),
        ),
        out_specs=(P(rows, None), P(rows, None), P("copies", None)),
        check_vma=False,
    )
```

```python
import functools
import jax
import jax.numpy as jnp
from jax import lax
from jax.experimental import pallas as pl
from jax.experimental.pallas import tpu as pltpu
from jax.sharding import PartitionSpec as P

F32 = jnp.float32
BF16 = jnp.bfloat16
VMEM = pl.BlockSpec(memory_space=pltpu.VMEM)
SMEM = pl.BlockSpec(memory_space=pltpu.SMEM)
HBM = pl.BlockSpec(memory_space=pltpu.HBM)
ANY = pl.BlockSpec(memory_space=pl.ANY)
PARAMS = pltpu.CompilerParams(vmem_limit_bytes=48 * 1024 * 1024)


def partner(i, k, n):
    if n & (n - 1) == 0:
        return i ^ k
    return (i + k) % n


def back_partner(i, k, n):
    if n & (n - 1) == 0:
        return i ^ k
    return (i + n - k) % n


def exchange_order(n):
    return sorted(range(1, n), key=lambda k: -k)


def send(x, axis, k, n):
    return lax.ppermute(x, axis, [(i, partner(i, k, n)) for i in range(n)])


def send_back(x, axis, k, n):
    return lax.ppermute(x, axis, [(i, back_partner(i, k, n)) for i in range(n)])


def split(x):
    hi = x.astype(BF16)
    return hi, (x - hi.astype(F32)).astype(BF16)


def mm(a, b, dims=((1,), (0,))):
    return lax.dot_general(a, b, (dims, ((), ())), preferred_element_type=F32)


def mm3(a, b, dims=((1,), (0,))):
    ah, al = a
    bh, bl = b
    return mm(ah, bh, dims) + (mm(ah, bl, dims) + mm(al, bh, dims))


def call(kernel, out_shape, flops, nbytes, in_specs, out_specs, scratch=(), aliases={}):
    return pl.pallas_call(
        kernel,
        out_shape=out_shape,
        in_specs=in_specs,
        out_specs=out_specs,
        scratch_shapes=list(scratch),
        input_output_aliases=aliases,
        compiler_params=PARAMS,
        cost_estimate=pl.CostEstimate(flops=flops, bytes_accessed=nbytes, transcendentals=0),
    )


def fetch(pairs, sems):
    copies = [pltpu.make_async_copy(src, dst, sems.at[i]) for i, (src, dst) in enumerate(pairs)]
    for copy in copies:
        copy.start()
    return copies


def pack_rows(out_ref, targets_ref, peer, rows_ref, side):
    for j in range(targets_ref.shape[1]):
        target = targets_ref[0, j, peer]
        rows = rows_ref[pl.ds(pl.multiple_of(jnp.maximum(target, 0) * side, side), side), :]
        out_ref[j * side : (j + 1) * side, :] = jnp.where(target >= 0, rows, 0.0).astype(BF16)


def pack_kernel(ns, nd, side, inner_hbm, outer_hbm, features_hbm, *refs):
    out_refs, (inner_ref, outer_ref, rows_ref, sems) = refs[:-4], refs[-4:]
    half = rows_ref.shape[0] // 2
    copies = fetch(
        [
            (inner_hbm, inner_ref),
            (outer_hbm, outer_ref),
            (features_hbm.at[:half], rows_ref.at[:half]),
            (features_hbm.at[half:], rows_ref.at[half:]),
        ],
        sems,
    )
    for copy in copies:
        copy.wait()
    s = lax.axis_index("shard")
    p = lax.axis_index("dom")
    plan = [(inner_ref, partner(s, k, ns)) for k in exchange_order(ns)]
    plan += [(outer_ref, partner(p, k, nd)) for k in exchange_order(nd)[:-1]]
    for out_ref, (targets_ref, peer) in zip(out_refs, plan):
        pack_rows(out_ref, targets_ref, peer, rows_ref, side)


def slot_codes(row_blocks, ns, nd, inner_cap, outer_cap):
    s = lax.axis_index("shard")
    p = lax.axis_index("dom")
    codes = []
    for k in exchange_order(ns):
        for j in range(inner_cap):
            codes.append(row_blocks + back_partner(s, k, ns) * inner_cap + j)
    for k in exchange_order(nd):
        for j in range(outer_cap):
            codes.append(row_blocks + ns * inner_cap + back_partner(p, k, nd) * outer_cap + j)
    return codes


def local_kernel(
    dims, list_hbm, outer_hbm, features_hbm, weight_hbm, values_hbm,
    near_ref, base_ref, local_ref, scale_ref, picked_ref, turned_ref, values_ref, place_ref,
    list_ref, outer_ref, features_ref, weight_ref, sources_ref, inverse_ref, sems,
):
    row_blocks, fanout, side, width, ns, nd, inner_cap, outer_cap = dims
    pairs = [
        (list_hbm, list_ref), (outer_hbm, outer_ref), (features_hbm, features_ref), (weight_hbm, weight_ref)
    ]
    pairs += [(values_hbm.at[r], values_ref.at[r]) for r in range(row_blocks)]
    copies = fetch(pairs, sems)
    for copy in copies[:4]:
        copy.wait()
    pack_rows(near_ref, outer_ref, partner(lax.axis_index("dom"), exchange_order(nd)[-1], nd), features_ref, side)
    codes = row_blocks + ns * inner_cap + nd * outer_cap
    for c in range(codes):
        inverse_ref[c] = 0
    for n in range(row_blocks * fanout):
        inverse_ref[list_ref[n // fanout, n % fanout]] = n
    fh, fl = split(features_ref[...])
    projected = mm3((fh, fl), split(weight_ref[...]))
    sources_ref[: row_blocks * side, :width] = projected.astype(BF16)
    sources_ref[: row_blocks * side, width : 2 * width] = fh
    sources_ref[: row_blocks * side, 2 * width :] = fl
    sources_ref[row_blocks * side :, :] = jnp.zeros((side, 3 * width), BF16)
    for copy in copies[4:]:
        copy.wait()
    for r in range(row_blocks):
        rows = slice(r * side, (r + 1) * side)
        squares = jnp.zeros((side, side), F32)
        for k in range(fanout):
            block = values_ref[r, k].astype(F32)
            squares = squares + block * block
        scale = lax.rsqrt(1.0 + jnp.sum(squares, axis=1, keepdims=True))
        scale_ref[rows, :] = jnp.broadcast_to(scale, (side, width))
        total = jnp.zeros((side, 3 * width), F32)
        for k in range(0, fanout, 2):
            blocks = jnp.concatenate([values_ref[r, k], values_ref[r, k + 1]], axis=1)
            picks = []
            for kk in (k, k + 1):
                at = pl.multiple_of(jnp.minimum(list_ref[r, kk], row_blocks) * side, side)
                picks.append(sources_ref[pl.ds(at, side), :])
            total = total + mm(blocks, jnp.concatenate(picks, axis=0))
        base_ref[rows, :] = projected[rows, :] + total[:, :width]
        local_ref[rows, :] = total[:, width : 2 * width] + total[:, 2 * width :]
    for i, code in enumerate(slot_codes(row_blocks, ns, nd, inner_cap, outer_cap)):
        n = inverse_ref[code]
        r = n // fanout
        place_ref[i] = r
        block = values_ref[r, n % fanout]
        picked_ref[i] = block
        turned_ref[i] = block.T


def middle_kernel(dims, place_any, *refs):
    row_blocks, fanout, side, width, ns, nd, inner_cap, outer_cap = dims
    n_in = (ns - 1) + (nd - 1)
    arrived = refs[:n_in]
    base_ref, scale_ref, picked_ref, turned_ref, weight_ref, cotangent_ref = refs[n_in : n_in + 6]
    mixed_ref, scaled_ref, half_ref, total_ref = refs[n_in + 6 : n_in + 10]
    leaving, (place_ref, sem) = refs[n_in + 10 : -2], refs[-2:]
    copy = pltpu.make_async_copy(place_any, place_ref, sem)
    copy.start()
    terms = []
    for ref in arrived:
        for j in range(ref.shape[0] // side):
            terms.append(mm(picked_ref[len(terms)], ref[j * side : (j + 1) * side, :]))
    total_ref[...] = jnp.zeros_like(total_ref)
    copy.wait()
    for i, term in enumerate(terms):
        rows = pl.ds(pl.multiple_of(place_ref[i] * side, side), side)
        total_ref[rows, :] += term
    weight = split(weight_ref[...])
    for r in range(row_blocks):
        rows = slice(r * side, (r + 1) * side)
        scale = scale_ref[rows, :]
        mixed = (base_ref[rows, :] + mm3(split(total_ref[rows, :]), weight)) * scale
        gate = jax.nn.sigmoid(mixed)
        mixed_ref[rows, :] = mixed
        scaled = cotangent_ref[rows, :] * gate * (1.0 + mixed * (1.0 - gate)) * scale
        scaled_ref[rows, :] = scaled
        half_ref[rows, :] = scaled.astype(BF16)
    i = 0
    for ref in leaving:
        for j in range(inner_cap):
            rows = pl.ds(pl.multiple_of(place_ref[i] * side, side), side)
            ref[j * side : (j + 1) * side, :] = mm(turned_ref[i], half_ref[rows, :]).astype(BF16)
            i += 1


def turn_rows(ref, place_ref, turned_ref, half_ref, first, count, side):
    for j in range(count):
        rows = pl.ds(pl.multiple_of(place_ref[first + j] * side, side), side)
        ref[j * side : (j + 1) * side, :] = mm(turned_ref[first + j], half_ref[rows, :]).astype(BF16)


def weight_kernel(
    dims, first, place_any, features_ref, local_ref, total_ref, scaled_ref, half_ref, turned_ref, own_ref, *refs
):
    row_blocks, fanout, side, width, ns, nd, inner_cap, outer_cap = dims
    leaving, (term_ref, place_ref, sem) = refs[:-3], refs[-3:]
    copy = pltpu.make_async_copy(place_any, place_ref, sem)
    copy.start()
    down = ((0,), (0,))
    ah, al = split(local_ref[...] + total_ref[...])
    half = half_ref[...]
    term = mm3(split(features_ref[...]), split(scaled_ref[...]), down)
    term_ref[...] = term + (mm(ah, half, down) + mm(al, half, down))
    count = own_ref.shape[0]
    mine = lax.axis_index("dom") & 1
    own_ref[...] = term_ref[pl.ds(pl.multiple_of(mine * count, 8), count), :]
    hi, lo = split(term_ref[pl.ds(pl.multiple_of((1 - mine) * count, 8), count), :])
    copy.wait()
    for i, ref in enumerate(leaving):
        turn_rows(ref, place_ref, turned_ref, half_ref, first + i * outer_cap, outer_cap, side)
    start = outer_cap * side
    leaving[-1][start : start + count, :] = hi
    leaving[-1][start + count :, :] = lo


def halve(rows, bit, own_ref, give_ref, total_ref):
    mine = (lax.axis_index("dom") >> bit) & 1
    own_ref[...] = total_ref[pl.ds(pl.multiple_of(mine * rows, 8), rows), :]
    give_ref[...] = total_ref[pl.ds(pl.multiple_of((1 - mine) * rows, 8), rows), :]


def near_sum_kernel(start, own_ref, load_ref, next_ref, give_ref, total_ref):
    count = own_ref.shape[0]
    hi = load_ref[start : start + count, :].astype(F32)
    total_ref[...] = own_ref[...] + (hi + load_ref[start + count :, :].astype(F32))
    halve(next_ref.shape[0], 1, next_ref, give_ref, total_ref)


def far_sum_kernel(bit, own_ref, load_ref, next_ref, give_ref, total_ref):
    total_ref[...] = own_ref[...] + load_ref[...]
    halve(next_ref.shape[0], bit, next_ref, give_ref, total_ref)


def last_sum_kernel(own_ref, load_ref, *refs):
    refs[-1][...] = (own_ref[...] + load_ref[...]).astype(BF16)


def shard_sum_kernel(ns, own_ref, *refs):
    terms = dict(zip([0] + exchange_order(ns), (own_ref, *refs)))
    refs[-1][...] = tree_sum([terms[k][...].astype(F32) for k in range(ns)])


def owned_piece(index, nd):
    bits = nd.bit_length() - 1
    return sum(((index >> bit) & 1) << (bits - 1 - bit) for bit in range(bits))


def place_kernel(nd, *refs):
    p = lax.axis_index("dom")
    rows = refs[0].shape[0]
    for ref, k in zip(refs, [0] + exchange_order(nd)):
        at = pl.multiple_of(owned_piece(partner(p, k, nd), nd) * rows, 8)
        refs[-1][pl.ds(at, rows), :] = ref[...]


def spread_kernel(
    dims, list_any, values_ref, mixed_ref, scaled_ref, half_ref, act_hbm, out_ref, act_ref, list_ref, sums_ref, sems
):
    row_blocks, fanout, side, width = dims
    (listed,) = fetch([(list_any, list_ref)], sems)
    mixed = mixed_ref[...]
    act_ref[...] = mixed * jax.nn.sigmoid(mixed)
    store = pltpu.make_async_copy(act_ref, act_hbm, sems.at[1])
    store.start()
    sums_ref[...] = jnp.zeros_like(sums_ref)
    listed.wait()
    for r in range(row_blocks):
        half = half_ref[r * side : (r + 1) * side, :].astype(F32).T.astype(BF16)
        for k in range(0, fanout, 2):
            blocks = jnp.concatenate([values_ref[r, k], values_ref[r, k + 1]], axis=1)
            terms = mm(half, blocks)
            for kk in (0, 1):
                sums_ref[jnp.minimum(list_ref[r, k + kk], row_blocks)] += terms[:, kk * side : (kk + 1) * side]
    for c in range(row_blocks):
        rows = slice(c * side, (c + 1) * side)
        out_ref[rows, :] = scaled_ref[rows, :] + sums_ref[c].T
    store.wait()


def tree_sum(terms):
    while len(terms) > 1:
        terms = [sum(terms[i : i + 2][1:], terms[i]) for i in range(0, len(terms), 2)]
    return terms[0]


def add_rows(sums_ref, ref, targets_ref, peer, side):
    for j in range(targets_ref.shape[1]):
        target = targets_ref[0, j, peer]
        rows = pl.ds(pl.multiple_of(jnp.maximum(target, 0) * side, side), side)
        term = ref[j * side : (j + 1) * side, :].astype(F32)
        sums_ref[rows, :] += jnp.where(target >= 0, term, 0.0)


def finish_kernel(items, sizes, side, inner_any, outer_any, part_ref, weight_ref, *refs):
    arrived, (out_hbm, out_ref, sums_ref, inner_ref, outer_ref, sems) = refs[:-6], refs[-6:]
    tables = fetch([(inner_any, inner_ref), (outer_any, outer_ref)], sems)
    sums_ref[...] = part_ref[...]
    weight = split(weight_ref[...])
    for copy in tables:
        copy.wait()
    for (axis, k), ref in zip(items, arrived):
        targets_ref = inner_ref if axis == "shard" else outer_ref
        add_rows(sums_ref, ref, targets_ref, partner(lax.axis_index(axis), k, sizes[axis]), side)
    stores = []
    for r in range(sums_ref.shape[0] // side):
        rows = slice(r * side, (r + 1) * side)
        out_ref[rows, :] = mm3(split(sums_ref[rows, :]), weight, ((1,), (1,)))
        stores.append(pltpu.make_async_copy(out_ref.at[rows], out_hbm.at[rows], sems.at[2 + r]))
        stores[-1].start()
    for store in stores:
        store.wait()


GATES = {'last': [('dom', 1), ('dom', 2), ('dom', 3), 'part'], 'shard': [('shard', 2), ('shard', 3), ('shard', 1)], 'place': ['finish']}


def on_device(features, weight, cotangent, block_values, block_list, send_inner, send_outer):
    keep = lambda x: pltpu.with_memory_space_constraint(x, pltpu.HBM)
    node_count, width = features.shape
    row_blocks, fanout, side, _ = block_values.shape
    ns = lax.axis_size("shard")
    nd = lax.axis_size("dom")
    inner_cap = send_inner.shape[2]
    outer_cap = send_outer.shape[2]
    slots = (ns - 1) * inner_cap + (nd - 1) * outer_cap
    dims = (row_blocks, fanout, side, width, ns, nd, inner_cap, outer_cap)
    shape = jax.ShapeDtypeStruct
    rows_f32 = shape((node_count, width), F32)
    rows_f16 = shape((node_count, width), BF16)
    packed_inner = [shape((inner_cap * side, width), BF16)] * (ns - 1)
    packed_outer = [shape((outer_cap * side, width), BF16)] * (nd - 1)
    nbytes = node_count * width * 4

    inner_targets = jnp.swapaxes(send_inner, 1, 2)
    outer_targets = jnp.swapaxes(send_outer, 1, 2)
    inner_table = pltpu.SMEM(inner_targets.shape, jnp.int32)
    outer_table = pltpu.SMEM(outer_targets.shape, jnp.int32)
    list_table = pltpu.SMEM(block_list.shape, jnp.int32)
    inner_order, outer_order = exchange_order(ns), exchange_order(nd)

    packed = call(
        functools.partial(pack_kernel, ns, nd, side), packed_inner + packed_outer[:-1], 0, 3 * nbytes,
        [HBM] * 3, [VMEM] * (ns - 1 + nd - 2),
        [inner_table, outer_table, pltpu.VMEM(features.shape, F32), pltpu.SemaphoreType.DMA((4,))],
    )(keep(inner_targets), keep(outer_targets), keep(features))
    inner_in = [send(x, "shard", k, ns) for x, k in zip(packed, inner_order)]
    outer_in = [send(x, "dom", k, nd) for x, k in zip(packed[ns - 1 :], outer_order)]

    near, base, local, scale, picked, turned, values, place = call(
        functools.partial(local_kernel, dims),
        [
            packed_outer[-1], rows_f32, rows_f32, rows_f32,
            shape((slots, side, side), BF16), shape((slots, side, side), BF16),
            shape(block_values.shape, BF16), shape((slots,), jnp.int32),
        ],
        4 * row_blocks * fanout * side * side * width * 3, 12 * nbytes,
        [HBM] * 5, [VMEM] * 7 + [SMEM],
        [
            list_table, outer_table, pltpu.VMEM(features.shape, F32), pltpu.VMEM(weight.shape, F32),
            pltpu.VMEM(((row_blocks + 1) * side, 3 * width), BF16),
            pltpu.SMEM((row_blocks + ns * inner_cap + nd * outer_cap,), jnp.int32),
            pltpu.SemaphoreType.DMA((4 + row_blocks,)),
        ],
    )(keep(block_list), keep(outer_targets), keep(features), keep(weight), keep(block_values))
    outer_in.append(send(near, "dom", outer_order[-1], nd))

    n_in = ns - 1 + nd - 1
    outs = call(
        functools.partial(middle_kernel, dims),
        [rows_f32, rows_f32, rows_f16, rows_f32] + packed_inner,
        2 * slots * side * side * width * 2, 8 * nbytes,
        [ANY] + [VMEM] * (n_in + 6), [VMEM] * (4 + ns - 1),
        [pltpu.SMEM((slots,), jnp.int32), pltpu.SemaphoreType.DMA],
    )(place, *inner_in, *outer_in, base, scale, picked, turned, weight, cotangent)
    mixed, scaled, half, total = outs[:4]
    inner_back = [send_back(x, "shard", k, ns) for x, k in zip(outs[4:], inner_order)]

    count = width // 2
    outs = call(
        functools.partial(weight_kernel, dims, (ns - 1) * inner_cap),
        [shape((count, width), F32)] + packed_outer[:-1] + [shape((outer_cap * side + 2 * count, width), BF16)],
        10 * node_count * width * width, 5 * nbytes,
        [ANY] + [VMEM] * 6, [VMEM] * nd,
        [pltpu.VMEM((width, width), F32), pltpu.SMEM((slots,), jnp.int32), pltpu.SemaphoreType.DMA],
    )(place, features, local, total, scaled, half, turned)
    own, outer_terms = outs[0], outs[1:]
    near_back = send_back(outer_terms[-1], "dom", 1, nd)
    outer_back = [send_back(x, "dom", k, nd) for x, k in zip(outer_terms[:-1], outer_order)] + [near_back]

    activations, part = call(
        functools.partial(spread_kernel, dims[:4]), [rows_f32, rows_f32],
        2 * row_blocks * fanout * side * side * width, 8 * nbytes,
        [ANY] + [VMEM] * 4, [HBM, VMEM],
        [
            pltpu.VMEM((node_count, width), F32), list_table, pltpu.VMEM((row_blocks + 1, width, side), F32),
            pltpu.SemaphoreType.DMA((2,)),
        ],
    )(block_list, values, mixed, scaled, half)

    back = {("shard", k): x for k, x in zip(inner_order, inner_back)}
    back.update({("dom", k): x for k, x in zip(outer_order, outer_back)})
    sizes = {"shard": ns, "dom": nd}

    grad_features = call(
        functools.partial(finish_kernel, list(back), sizes, side), rows_f32,
        6 * node_count * width * width, 4 * nbytes, [ANY] * 2 + [VMEM] * (2 + len(back)), HBM,
        [
            pltpu.VMEM((node_count, width), F32), pltpu.VMEM((node_count, width), F32), inner_table, outer_table,
            pltpu.SemaphoreType.DMA((2 + row_blocks,)),
        ],
    )(inner_targets, outer_targets, part, weight, *back.values())
    back["part"] = part
    back["finish"] = keep(grad_features)

    def stage(kernel, name, inputs, rows, dtype=F32):
        gated = [back[item] for item in GATES.get(name, ()) if item in back]
        return call(
            kernel, shape((rows, width), dtype), 0, nbytes // 4,
            [VMEM] * len(inputs) + [ANY] * len(gated), VMEM,
        )(*inputs, *gated)

    bits = nd.bit_length() - 1
    load = near_back
    for bit in range(bits):
        if bit == bits - 1:
            piece = stage(last_sum_kernel, "last", [own, load], count, BF16)
            break
        kernel = functools.partial(near_sum_kernel, outer_cap * side) if bit == 0 else functools.partial(far_sum_kernel, bit + 1)
        count //= 2
        own, give = call(
            kernel, [shape((count, width), F32)] * 2, 0, nbytes // 4,
            [VMEM] * 2, [VMEM] * 2, [pltpu.VMEM((2 * count, width), F32)],
        )(own, load)
        load = send(give, "dom", 2 << bit, nd)
    pieces = [piece] + [send(piece, "shard", k, ns) for k in inner_order]
    weight_sum = stage(functools.partial(shard_sum_kernel, ns), "shard", pieces, count)
    pieces = [weight_sum] + [send(weight_sum, "dom", k, nd) for k in outer_order]
    weight_sum = stage(functools.partial(place_kernel, nd), "place", pieces, width)
    grad_weight = weight_sum
    return (activations, grad_features, grad_weight)


def solution(mesh):
    rows = ("copies", "shard", "dom")
    return jax.shard_map(
        on_device,
        mesh=mesh,
        in_specs=(
            P(rows, None),
            P(),
            P(rows, None),
            P(rows, None, None, None),
            P(rows, None),
            P(rows, None, None),
            P(rows, None, None),
        ),
        out_specs=(P(rows, None), P(rows, None), P("copies", None)),
        check_vma=False,
    )
```
